512 devices in a mesh: dp: 8 (over y), expert: 64 (over z, x, core).
Axes of the slice: x: 4, y: 8, z: 8, core: 2. Of those that a mesh axis runs over, the one named last changes fastest.
Arguments:
- tokens: bfloat16 [65536, 4096], P(('dp', 'expert')), may hold values from -6 to 6
- routes: int32 [65536, 8], P(('dp', 'expert')), may hold values from 0 to 63, all different within a row; in each aligned block of 128 rows (0 to 127, 128 to 255, ...) at most 20 rows name the same one
- mix_weights: float32 [65536, 8], P(('dp', 'expert')), may hold values from 0.05 to 0.45
- gate_up: bfloat16 [64, 512, 1024], P('expert'), may hold values from -0.25 to 0.25
- down: bfloat16 [64, 512, 512], P('expert'), may hold values from -0.25 to 0.25
- w_in: bfloat16 [4096, 512], P(('dp', 'expert')), may hold values from -0.09375 to 0.09375
- grad_combined: bfloat16 [65536, 512], P(('dp', 'expert')), may hold values from -6 to 6
Outputs:
- combined: bfloat16 [65536, 512], P(('dp', 'expert'))
- grad_tokens: bfloat16 [65536, 4096], P(('dp', 'expert'))
- grad_w_in: float32 [4096, 512], P(('dp', 'expert'))
The draws below stay inside these ranges and needn't reach their ends.
Inputs may be any that keep to these rules, and one draw needn't show every extreme that they name: `routes`: each row names 8 different experts. Among the rows of one device no expert is named more than 20 times, and in every draw some expert is named exactly 20 times by some device's rows.
All inputs are finite; a program needn't handle non-finite values.
Results may differ from the reference program's by a relative error of at most 0.0085.
Values may be sent and summed in bfloat16 or wider, within the bound.
No kernel may reach another device: no remote copies, remote signals or barrier semaphores. Data moves between devices by JAX's collectives and lax.ppermute only.
A program may use at most 64 MiB of HBM per device.

```python
import math
import jax
import jax.numpy as jnp
import numpy as np
from jax import lax

D = 4096
L = 512
FF = 512
TOP = 8
TOK_DEV = 128
EXPERTS = 64
CAP = 20
TOKENS = 65536
N_DP = 8
N_EXPERT = 64


def block_levels(key, dims, cuts, least, top_value):
    level = 1.0
    for axis_at, blocks in cuts:
        heights = jax.random.uniform(jax.random.fold_in(jax.random.fold_in(key, 6), axis_at), (blocks,), jnp.float32, least / len(cuts), top_value / len(cuts))
        level = level * jnp.repeat(jnp.exp(heights), dims[axis_at] // blocks).reshape((-1,) + (1,) * (len(dims) - 1 - axis_at))
    return level


def deal_out(stream_key, own, number, rows, amount, top, reach, lean):
    order = jax.random.permutation(stream_key, amount)
    heavy_load, ordinary = load_shares(amount, rows * top, reach, lean, True), load_shares(amount, rows * top, reach, lean, False)
    places = jnp.arange(amount)

    def named(sizes, turn):
        used = int((sizes > 0).sum())
        fixed = max(1, used // 4)
        passed = fixed + (places - fixed + turn * (used - fixed)) % max(1, amount - fixed)
        return jnp.zeros((amount,), jnp.int32).at[order[jnp.where(places < fixed, places, passed)]].set(jnp.asarray(sizes, jnp.int32))

    sizes = jnp.where(number % 4 == 0, named(heavy_load, number // 4), named(ordinary, number - number // 4 - 1))
    mixed = jax.random.permutation(jax.random.fold_in(own, 3), amount)
    giver, receiver = mixed[0:amount // 2 * 2:2], mixed[1:amount // 2 * 2:2]
    room = jnp.minimum(sizes[giver] - 1, reach - sizes[receiver]) // 2
    room = jnp.where((giver == order[0]) | (receiver == order[0]) | (sizes[receiver] == 0), 0, jnp.maximum(room, 0))
    passed = jax.random.randint(jax.random.fold_in(own, 4), (amount // 2,), 0, 1 << 20) % (room + 1)
    sizes = sizes.at[giver].add(-passed).at[receiver].add(passed)
    labels = jnp.searchsorted(jnp.cumsum(sizes), jnp.arange(rows * top), side="right").astype(jnp.int32)
    listing = labels.reshape(top, rows).T
    listing = listing[jax.random.permutation(jax.random.fold_in(own, 1), rows)]
    turn = jax.random.randint(jax.random.fold_in(own, 2), (rows, 1), 0, top)
    return jnp.take_along_axis(listing, (jnp.arange(top)[None, :] + turn) % top, axis=1)


def load_shares(amount, total, bound, slope, full):
    weights = [(1 << 20) // math.isqrt(rank ** slope) + 1 for rank in range(1, amount + 1)]
    largest = bound if full else min(bound, max(-(-total // amount), total * weights[0] // sum(weights)))
    least = 1 if total - largest >= amount - 1 else 0
    given, surplus = [largest] + [least] * (amount - 1), total - largest - least * (amount - 1)
    while surplus > 0:
        free = [i for i in range(1, amount) if given[i] < largest] or [i for i in range(1, amount) if given[i] < bound]
        pool, left = sum([weights[i] for i in free]), surplus
        for i in free:
            extra = min(bound - given[i], max(1, left * weights[i] // pool), surplus)
            given[i] = given[i] + extra
            surplus = surplus - extra
    return np.array(given)


def scatter_about(own_key, shape, spread, most, pieces=(), held_as=jnp.bfloat16):
    array = jax.random.normal(own_key, shape, jnp.float32) * spread
    if len(pieces) > 0:
        array = block_levels(own_key, shape, pieces, -0.22, 0.18) * array
    return jnp.clip(array, min=-most, max=most).astype(held_as)


def setup_inputs(seed: int = 0) -> dict:
    keys = jax.random.split(jax.random.key(seed), 8)
    tokens = scatter_about(keys[0], (TOKENS, D), 1.0, 6.0, ((0, 512),))
    routes_keys = jax.random.split(jax.random.fold_in(keys[1], 1), TOKENS // TOK_DEV)
    routes_turns = jax.random.permutation(jax.random.fold_in(keys[1], 3), TOKENS // TOK_DEV)
    routes = jax.vmap(lambda own, number: deal_out(jax.random.fold_in(keys[1], 2), own, number, TOK_DEV, EXPERTS, TOP, CAP, 2))(routes_keys, routes_turns).reshape((TOKENS, TOP))
    mix_weights = jnp.clip(0.05 + 0.39999999 * jax.random.uniform(keys[2], (TOKENS, TOP), jnp.float32) ** block_levels(keys[2], (TOKENS, TOP), ((0, 512),), -0.2, 0.2), 0.05, 0.45)
    gate_up = scatter_about(keys[3], (EXPERTS, L, 2 * FF), L ** -0.5, 0.25, ((0, 64),))
    down = scatter_about(keys[4], (EXPERTS, FF, L), FF ** -0.5, 0.25, ((0, 64),))
    w_in = scatter_about(keys[5], (D, L), D ** -0.5, 0.09375, ((0, 512),))
    grad_combined = scatter_about(keys[6], (TOKENS, L), 1.0, 6.0, ((0, 512),))
    return dict(tokens=tokens, routes=routes, mix_weights=mix_weights, gate_up=gate_up, down=down, w_in=w_in, grad_combined=grad_combined)


def reference(tokens, routes, mix_weights, gate_up, down, w_in, grad_combined):
    latent = jnp.dot(tokens, w_in, preferred_element_type=jnp.float32).astype(jnp.bfloat16)
    flat = routes.reshape(-1).astype(jnp.int32)
    weights_flat = mix_weights.reshape(-1)
    order = jnp.argsort(flat, stable=True).astype(jnp.int32)
    counts = jnp.bincount(flat, length=EXPERTS).astype(jnp.int32)
    starts = (jnp.cumsum(counts) - counts).astype(jnp.int32)
    most = N_DP * N_EXPERT * CAP
    padded = jnp.concatenate([order, jnp.zeros((most,), jnp.int32)])
    latent_w = w_in.shape[1]
    hidden = down.shape[1]

    def per_expert(carry, expert_id):
        comb, glat = carry
        index = lax.dynamic_slice_in_dim(padded, starts[expert_id], most)
        valid = jnp.arange(most, dtype=jnp.int32) < counts[expert_id]
        token_ids = (index // TOP).astype(jnp.int32)
        weight = jnp.where(valid, weights_flat[index], jnp.zeros((), weights_flat.dtype))
        rows_in = latent[token_ids]
        w_gate = gate_up[expert_id]
        w_down = down[expert_id]
        pre = jnp.dot(rows_in, w_gate, preferred_element_type=jnp.float32)
        gate = pre[:, :hidden]
        upper = pre[:, hidden:]
        act = (jax.nn.silu(gate) * upper).astype(jnp.bfloat16)
        out = jnp.dot(act, w_down, preferred_element_type=jnp.float32).astype(jnp.bfloat16)
        comb = comb.at[token_ids].add(weight[:, None] * out.astype(jnp.float32))
        gslot = (weight[:, None] * grad_combined[token_ids].astype(jnp.float32)).astype(jnp.bfloat16)
        grad_act = jnp.dot(gslot, w_down.T, preferred_element_type=jnp.float32)
        sig = jax.nn.sigmoid(gate)
        grad_gate = grad_act * upper * sig * (1.0 + gate * (1.0 - sig))
        grad_up = grad_act * (gate * sig)
        grad_pre = jnp.concatenate([grad_gate, grad_up], axis=-1).astype(jnp.bfloat16)
        grad_rows = jnp.dot(grad_pre, w_gate.T, preferred_element_type=jnp.float32).astype(jnp.bfloat16)
        glat = glat.at[token_ids].add(jnp.where(valid[:, None], grad_rows.astype(jnp.float32), jnp.zeros((), jnp.float32)))
        return (comb, glat), None

    start_carry = (jnp.zeros((tokens.shape[0], latent_w), jnp.float32), jnp.zeros((tokens.shape[0], latent_w), jnp.float32))
    (comb, glat), unused = lax.scan(per_expert, start_carry, jnp.arange(EXPERTS, dtype=jnp.int32))
    combined = comb.astype(jnp.bfloat16)
    grad_latent = glat.astype(jnp.bfloat16)
    grad_tokens = lax.dot_general(grad_latent, w_in, (((1,), (1,)), ((), ())), preferred_element_type=jnp.float32).astype(jnp.bfloat16)
    grad_w_in = lax.dot_general(tokens, grad_latent, (((0,), (0,)), ((), ())), preferred_element_type=jnp.float32) / TOK_DEV
    return combined, grad_tokens, grad_w_in
```

```python
import jax
import jax.numpy as jnp
from jax import lax
from jax.sharding import Mesh, PartitionSpec as P

BF = jnp.bfloat16
F32 = jnp.float32
XC = ("x", "c")
YZ = ("dp", "z")
ZX = ("z", "x")
CAP = 20
MAIN = 16
PAIR = 2 * CAP


def mm(a, b, dims=((1,), (0,))):
    return lax.dot_general(a, b, (dims, ((), ())), preferred_element_type=F32)


def after(x, *deps):
    return lax.optimization_barrier((x,) + deps)[0]


def swap_core(x):
    return lax.ppermute(x, "c", [(0, 1), (1, 0)])


def column_order(tokens):
    rows = tokens.shape[0]
    a = lax.broadcasted_iota(jnp.int32, (1024, 1024), 0)
    b = lax.broadcasted_iota(jnp.int32, (1024, 1024), 1)
    y, z, xc, i = a // 512, (a // 64) % 8, (a // 8) % 8, a % 8
    pick = (xc * 128 + y * 64 + z * 8 + i == b).astype(BF)
    parts = [mm(tokens[:, p * 1024 : (p + 1) * 1024], pick).astype(BF) for p in range(4)]
    return jnp.concatenate(
        [parts[p][:, xc * 128 : (xc + 1) * 128] for xc in range(8) for p in range(4)], axis=1
    )


def shards(tokens, routes, mix_weights, gate_up, down, w_in, grad_combined):
    rows = tokens.shape[0]
    gate_up, down = gate_up[0], down[0]
    hidden = down.shape[0]
    experts = 64
    slots = experts * CAP

    w_part = lax.all_to_all(
        jnp.broadcast_to(w_in[None], (64,) + w_in.shape), YZ, split_axis=0, concat_axis=0, tiled=True
    ).reshape(512, 512)
    w_all = lax.all_gather(w_part, XC, axis=0, tiled=True)

    gate_up2, down2 = swap_core(gate_up), swap_core(down)

    core = lax.axis_index("c")
    r = lax.broadcasted_iota(jnp.int32, (experts, slots), 1)
    q = r % PAIR
    other = jnp.where(q < 2 * MAIN, q // MAIN, (q - 2 * MAIN) // (CAP - MAIN))
    spread = (
        lax.broadcasted_iota(jnp.int32, (experts, slots), 0) == (r // PAIR) * 2 + (core + other) % 2
    )
    q1 = lax.broadcasted_iota(jnp.int32, (rows, slots), 1) % PAIR
    place = jnp.where(q1 < 2 * MAIN, q1 % MAIN, MAIN + (q1 - 2 * MAIN) % (CAP - MAIN))
    hit = routes[:, :, None] == lax.broadcasted_iota(jnp.int32, (1, 1, experts), 2)
    named = jnp.any(hit, axis=1)
    weight = jnp.sum(jnp.where(hit, mix_weights[:, :, None], 0.0), axis=1)
    below = (
        lax.broadcasted_iota(jnp.int32, (rows, rows), 0)
        > lax.broadcasted_iota(jnp.int32, (rows, rows), 1)
    ).astype(BF)
    rank = mm(below, named.astype(BF))
    code = jnp.where(named, rank, -1.0).astype(BF)
    send = mm(code, spread.astype(BF)) == place.astype(F32)
    onehot = send.astype(BF)
    weight_hi = weight.astype(BF)
    weight_mid = (weight - weight_hi.astype(F32)).astype(BF)
    weight_lo = (weight - weight_hi.astype(F32) - weight_mid.astype(F32)).astype(BF)
    spread = spread.astype(BF)
    at_slot = mm(weight_hi, spread) + mm(weight_mid, spread) + mm(weight_lo, spread)
    weight_slot = jnp.where(send, at_slot, 0.0)
    slot_weight = jnp.sum(weight_slot, axis=0)
    mix_hi = weight_slot.astype(BF)
    mix_lo = (weight_slot - mix_hi.astype(F32)).astype(BF)

    picked = mm(onehot, grad_combined, ((0,), (0,)))
    grad_send = (slot_weight[:, None] * picked).astype(BF).reshape(32, PAIR, 512)
    grad_send = after(grad_send, w_part)
    grad_recv = lax.all_to_all(grad_send, ZX, split_axis=0, concat_axis=0, tiled=True)

    ordered = column_order(tokens)
    latent = mm(ordered, w_all).astype(BF)
    out_send = mm(onehot, latent, ((0,), (0,))).astype(BF).reshape(32, PAIR, 512)
    out_send = after(out_send, grad_recv)
    recv = lax.all_to_all(out_send, ZX, split_axis=0, concat_axis=0, tiled=True)

    feats = ordered.reshape(rows, 8, 512).transpose(1, 0, 2)
    feats = after(feats, recv)
    feature_block = lax.all_to_all(feats, XC, split_axis=0, concat_axis=0, tiled=True).reshape(
        8 * rows, 512
    )

    def split(x):
        tail = x[:, 2 * MAIN :].reshape(256, 512)
        return (
            jnp.concatenate([x[:, :MAIN].reshape(512, 512), tail]),
            jnp.concatenate([x[:, MAIN : 2 * MAIN].reshape(512, 512), tail]),
        )

    def join(a, b):
        own = (lax.broadcasted_iota(jnp.int32, (256, 1), 0) % 8) < 4
        tail = jnp.where(own, a[512:], b[512:])
        return jnp.concatenate(
            [a[:512].reshape(32, MAIN, 512), b[:512].reshape(32, MAIN, 512), tail.reshape(32, 8, 512)],
            axis=1,
        )

    def expert(x, g, w_up, w_down):
        pre = mm(x, w_up)
        gate, upper = pre[:, :hidden], pre[:, hidden:]
        sigma = jax.nn.sigmoid(gate)
        act = (gate * sigma * upper).astype(BF)
        grad_act = mm(g, w_down, ((1,), (1,)))
        grad_gate = grad_act * upper * sigma * (1.0 + gate * (1.0 - sigma))
        grad_up = grad_act * (gate * sigma)
        grad_pre = jnp.concatenate([grad_gate, grad_up], axis=-1).astype(BF)
        grad_rows = mm(grad_pre, w_up, ((1,), (1,))).astype(BF)
        out = mm(act, w_down).astype(BF)
        return out, grad_rows

    x1, x2 = split(recv)
    g1, g2 = split(grad_recv)
    o1, b1 = expert(x1, g1, gate_up, down)
    o2, b2 = expert(x2, g2, gate_up2, down2)
    grad_rows = after(join(b1, b2), feature_block)
    grad_back = lax.all_to_all(grad_rows, ZX, split_axis=0, concat_axis=0, tiled=True)
    outputs = after(join(o1, o2), grad_back)
    returned = lax.all_to_all(outputs, ZX, split_axis=0, concat_axis=0, tiled=True)

    grad_latent = mm(onehot, grad_back.reshape(slots, 512)).astype(BF)
    group_grads = lax.all_gather(grad_latent, XC, axis=0, tiled=True)
    part = mm(feature_block, group_grads, ((0,), (0,))).astype(BF).reshape(64, 8, 512)
    part = after(part, returned)
    parts = lax.all_to_all(part, YZ, split_axis=0, concat_axis=0, tiled=True)
    grad_w_in = jnp.sum(parts.astype(F32), axis=0) / rows

    w_natural = w_all.reshape(8, 64, 8, 512).transpose(1, 0, 2, 3).reshape(4096, 512)
    grad_tokens = mm(grad_latent, w_natural, ((1,), (1,))).astype(BF)
    flat = returned.reshape(slots, 512)
    combined = (mm(mix_hi, flat) + mm(mix_lo, flat)).astype(BF)
    return combined, grad_tokens, grad_w_in


def solution(mesh):
    split = Mesh(mesh.devices.reshape(8, 8, 4, 2), ("dp", "z", "x", "c"))
    every = P(("dp", "z", "x", "c"), None)
    each = P(("z", "x", "c"), None, None)
    return jax.shard_map(
        shards,
        mesh=split,
        in_specs=(every, every, every, each, each, every, every),
        out_specs=(every, every, every),
        check_vma=False,
    )
```

```python
import jax
import jax.numpy as jnp
from jax import lax
from jax.experimental import pallas as pl
from jax.experimental.pallas import tpu as pltpu
from jax.sharding import Mesh, PartitionSpec as P

BF = jnp.bfloat16
F32 = jnp.float32
XC = ("x", "c")
YZ = ("dp", "z")
ZX = ("z", "x")
CAP = 20
MAIN = 16
PAIR = 2 * CAP


def mm(a, b, dims=((1,), (0,))):
    return lax.dot_general(a, b, (dims, ((), ())), preferred_element_type=F32)


def after(x, *deps):
    return lax.optimization_barrier((x,) + deps)[0]


def swap_core(x):
    return lax.ppermute(x, "c", [(0, 1), (1, 0)])


def column_order(tokens):
    rows = tokens.shape[0]
    a = lax.broadcasted_iota(jnp.int32, (1024, 1024), 0)
    b = lax.broadcasted_iota(jnp.int32, (1024, 1024), 1)
    y, z, xc, i = a // 512, (a // 64) % 8, (a // 8) % 8, a % 8
    pick = (xc * 128 + y * 64 + z * 8 + i == b).astype(BF)
    parts = [mm(tokens[:, p * 1024 : (p + 1) * 1024], pick).astype(BF) for p in range(4)]
    return jnp.concatenate(
        [parts[p][:, xc * 128 : (xc + 1) * 128] for xc in range(8) for p in range(4)], axis=1
    )


def expert_kernel(x_ref, g_ref, up_ref, down_ref, back_ref, out_ref):
    w_up, w_down = up_ref[0], down_ref[0]
    x = x_ref[...].reshape(256, 512)
    g = g_ref[...].reshape(256, 512)
    pre = mm(x, w_up)
    grad_act = mm(g, w_down, ((1,), (1,)))
    gate, upper = pre[:, :512], pre[:, 512:]
    sigma = jax.nn.sigmoid(gate)
    soft = gate * sigma
    act = (soft * upper).astype(BF)
    grad_gate = (grad_act * upper * sigma * (1.0 + gate * (1.0 - sigma))).astype(BF)
    grad_up = (grad_act * soft).astype(BF)
    last = ((1,), (1,))
    back = mm(grad_gate, w_up[:, :512], last) + mm(grad_up, w_up[:, 512:], last)
    back = back.astype(BF).reshape(16, 16, 512)
    out = mm(act, w_down).astype(BF).reshape(16, 16, 512)
    step = pl.program_id(0)

    @pl.when(step != 3)
    def _():
        back_ref[...] = back
        out_ref[...] = out

    @pl.when(step == 3)
    def _():
        keep = (lax.broadcasted_iota(jnp.int32, (16, 16, 512), 1) % 8) < 4
        back_ref[...] = jnp.where(keep, back_ref[...].astype(F32), back.astype(F32)).astype(BF)
        out_ref[...] = jnp.where(keep, out_ref[...].astype(F32), out.astype(F32)).astype(BF)


def expert_rows(x, g, ups, downs):
    def block(i):
        return (0, jnp.where(i == 0, 0, jnp.where(i == 1, 3, jnp.where(i < 4, 2, jnp.where(i == 4, 1, 4)))), 0)

    rows = pl.BlockSpec((16, 16, 512), block)
    shape = jax.ShapeDtypeStruct((16, 80, 512), BF)
    back, out = pl.pallas_call(
        expert_kernel,
        grid=(6,),
        in_specs=[
            rows,
            rows,
            pl.BlockSpec((1, 512, 1024), lambda i: (i // 3, 0, 0)),
            pl.BlockSpec((1, 512, 512), lambda i: (i // 3, 0, 0)),
        ],
        out_specs=[rows, rows],
        out_shape=[shape, shape],
        compiler_params=pltpu.CompilerParams(vmem_limit_bytes=40 * 1024 * 1024),
        cost_estimate=pl.CostEstimate(flops=4_800_000_000, bytes_accessed=8_500_000, transcendentals=800_000),
    )(x.reshape(16, 80, 512), g.reshape(16, 80, 512), ups, downs)
    return back.reshape(32, PAIR, 512), out.reshape(32, PAIR, 512)


def shards(tokens, routes, mix_weights, gate_up, down, w_in, grad_combined):
    rows = tokens.shape[0]
    gate_up, down = gate_up[0], down[0]
    experts = 64
    slots = experts * CAP

    w_part = lax.all_to_all(
        jnp.broadcast_to(w_in[None], (64,) + w_in.shape), YZ, split_axis=0, concat_axis=0, tiled=True
    ).reshape(512, 512)
    w_all = lax.all_gather(w_part, XC, axis=0, tiled=True)

    gate_up2, down2 = swap_core(gate_up), swap_core(down)

    core = lax.axis_index("c")
    shift = 32 * (lax.axis_index("x") % 2)
    r = lax.broadcasted_iota(jnp.int32, (experts, slots), 1)
    q = (r % PAIR + shift) % PAIR
    other = jnp.where(q < 2 * MAIN, q // MAIN, (q - 2 * MAIN) // (CAP - MAIN))
    spread = (
        lax.broadcasted_iota(jnp.int32, (experts, slots), 0) == (r // PAIR) * 2 + (core + other) % 2
    )
    q1 = (lax.broadcasted_iota(jnp.int32, (rows, slots), 1) % PAIR + shift) % PAIR
    place = jnp.where(q1 < 2 * MAIN, q1 % MAIN, MAIN + (q1 - 2 * MAIN) % (CAP - MAIN))
    hit = routes[:, :, None] == lax.broadcasted_iota(jnp.int32, (1, 1, experts), 2)
    named = jnp.any(hit, axis=1)
    weight = jnp.sum(jnp.where(hit, mix_weights[:, :, None], 0.0), axis=1)
    below = (
        lax.broadcasted_iota(jnp.int32, (rows, rows), 0)
        > lax.broadcasted_iota(jnp.int32, (rows, rows), 1)
    ).astype(BF)
    rank = mm(below, named.astype(BF))
    code = jnp.where(named, rank, -1.0).astype(BF)
    send = mm(code, spread.astype(BF)) == place.astype(F32)
    onehot = send.astype(BF)
    weight_hi = weight.astype(BF)
    weight_mid = (weight - weight_hi.astype(F32)).astype(BF)
    weight_lo = (weight - weight_hi.astype(F32) - weight_mid.astype(F32)).astype(BF)
    spread = spread.astype(BF)
    at_slot = mm(weight_hi, spread) + mm(weight_mid, spread) + mm(weight_lo, spread)
    weight_slot = jnp.where(send, at_slot, 0.0)
    slot_weight = jnp.sum(weight_slot, axis=0)
    mix_hi = weight_slot.astype(BF)
    mix_lo = (weight_slot - mix_hi.astype(F32)).astype(BF)

    picked = mm(onehot, grad_combined, ((0,), (0,)))
    grad_send = (slot_weight[:, None] * picked).astype(BF).reshape(32, PAIR, 512)
    grad_send = after(grad_send, w_part)
    grad_recv = lax.all_to_all(grad_send, ZX, split_axis=0, concat_axis=0, tiled=True)

    ordered = column_order(tokens)
    latent = mm(ordered, w_all).astype(BF)
    out_send = mm(onehot, latent, ((0,), (0,))).astype(BF).reshape(32, PAIR, 512)
    out_send = after(out_send, grad_recv)
    recv = lax.all_to_all(out_send, ZX, split_axis=0, concat_axis=0, tiled=True)

    me, other_core = core, 1 - core
    feats = ordered.reshape(rows, 4, 2, 512).transpose(2, 1, 0, 3)
    mine = lax.dynamic_index_in_dim(feats, me, 0, keepdims=False)
    theirs = swap_core(lax.dynamic_index_in_dim(feats, other_core, 0, keepdims=False))
    both = jnp.stack([mine, theirs], axis=1)
    at = lax.axis_index("x")
    blocks = [lax.dynamic_index_in_dim(both, at, 0, keepdims=False)]
    for d in (1, 2, 3):
        block = lax.dynamic_index_in_dim(both, (at + d) % 4, 0, keepdims=False)
        blocks.append(lax.ppermute(block, "x", [(i, (i + d) % 4) for i in range(4)]))
    blocks = jnp.stack(blocks)
    feature_block = jnp.stack(
        [lax.dynamic_index_in_dim(blocks, (at - j) % 4, 0, keepdims=False) for j in range(4)], axis=1
    ).reshape(2, 4 * rows, 512)

    ups = jnp.stack([gate_up, gate_up2])
    downs = jnp.stack([down, down2])
    grad_rows, outputs = expert_rows(recv, grad_recv, ups, downs)
    grad_back = lax.all_to_all(grad_rows, ZX, split_axis=0, concat_axis=0, tiled=True)
    outputs = after(outputs, grad_back)
    returned = lax.all_to_all(outputs, ZX, split_axis=0, concat_axis=0, tiled=True)

    grad_latent = mm(onehot, grad_back.reshape(slots, 512)).astype(BF)
    line_grads = lax.all_gather(grad_latent, "x", axis=0, tiled=True)
    other_grads = swap_core(line_grads)
    first = ((0,), (0,))
    part = mm(feature_block[0], line_grads, first) + mm(feature_block[1], other_grads, first)
    part = part.astype(BF).reshape(64, 8, 512)
    part = after(part, returned)
    parts = lax.all_to_all(part, YZ, split_axis=0, concat_axis=0, tiled=True)
    grad_w_in = jnp.sum(parts.astype(F32), axis=0) / rows

    w_natural = w_all.reshape(8, 64, 8, 512).transpose(1, 0, 2, 3).reshape(4096, 512)
    grad_tokens = mm(grad_latent, w_natural, ((1,), (1,))).astype(BF)
    flat = returned.reshape(slots, 512)
    combined = (mm(mix_hi, flat) + mm(mix_lo, flat)).astype(BF)
    return combined, grad_tokens, grad_w_in


def solution(mesh):
    split = Mesh(mesh.devices.reshape(8, 8, 4, 2), ("dp", "z", "x", "c"))
    every = P(("dp", "z", "x", "c"), None)
    each = P(("z", "x", "c"), None, None)
    return jax.shard_map(
        shards,
        mesh=split,
        in_specs=(every, every, every, each, each, every, every),
        out_specs=(every, every, every),
        check_vma=False,
    )
```

```python
import jax
import jax.numpy as jnp
from jax import lax
from jax.experimental import pallas as pl
from jax.experimental.pallas import tpu as pltpu
from jax.sharding import Mesh, PartitionSpec as P

BF = jnp.bfloat16
F32 = jnp.float32
XC = ("x", "c")
YZ = ("dp", "z")
ZX = ("z", "x")
CAP = 20
MAIN = 16
PAIR = 2 * CAP


def mm(a, b, dims=((1,), (0,))):
    return lax.dot_general(a, b, (dims, ((), ())), preferred_element_type=F32)


def after(x, *deps):
    return lax.optimization_barrier((x,) + deps)[0]


def swap_core(x):
    return lax.ppermute(x, "c", [(0, 1), (1, 0)])


def column_order(tokens):
    a = lax.broadcasted_iota(jnp.int32, (1024, 1024), 0)
    b = lax.broadcasted_iota(jnp.int32, (1024, 1024), 1)
    y, z, xc, i = a // 512, (a // 64) % 8, (a // 8) % 8, a % 8
    pick = (xc * 128 + y * 64 + z * 8 + i == b).astype(BF)
    parts = [mm(tokens[:, p * 1024 : (p + 1) * 1024], pick).astype(BF) for p in range(4)]
    return jnp.concatenate(
        [parts[p][:, xc * 128 : (xc + 1) * 128] for xc in range(8) for p in range(4)], axis=1
    )


def expert_kernel(x_ref, g_ref, up_ref, down_ref, back_ref, out_ref):
    w_up, w_down = up_ref[0], down_ref[0]
    x = x_ref[...].reshape(256, 512)
    g = g_ref[...].reshape(256, 512)
    pre = mm(x, w_up)
    grad_act = mm(g, w_down, ((1,), (1,)))
    gate, upper = pre[:, :512], pre[:, 512:]
    sigma = jax.nn.sigmoid(gate)
    soft = gate * sigma
    act = (soft * upper).astype(BF)
    grad_gate = (grad_act * upper * sigma * (1.0 + gate * (1.0 - sigma))).astype(BF)
    grad_up = (grad_act * soft).astype(BF)
    last = ((1,), (1,))
    back = mm(grad_gate, w_up[:, :512], last) + mm(grad_up, w_up[:, 512:], last)
    back = back.astype(BF).reshape(16, 16, 512)
    out = mm(act, w_down).astype(BF).reshape(16, 16, 512)
    step = pl.program_id(0)

    @pl.when(step != 3)
    def _():
        back_ref[...] = back
        out_ref[...] = out

    @pl.when(step == 3)
    def _():
        keep = (lax.broadcasted_iota(jnp.int32, (16, 16, 512), 1) % 8) < 4
        back_ref[...] = jnp.where(keep, back_ref[...].astype(F32), back.astype(F32)).astype(BF)
        out_ref[...] = jnp.where(keep, out_ref[...].astype(F32), out.astype(F32)).astype(BF)


def expert_rows(x, g, ups, downs):
    def block(i):
        return (0, jnp.where(i == 0, 0, jnp.where(i == 1, 3, jnp.where(i < 4, 2, jnp.where(i == 4, 1, 4)))), 0)

    rows = pl.BlockSpec((16, 16, 512), block)
    shape = jax.ShapeDtypeStruct((16, 80, 512), BF)
    back, out = pl.pallas_call(
        expert_kernel,
        grid=(6,),
        in_specs=[
            rows,
            rows,
            pl.BlockSpec((1, 512, 1024), lambda i: (i // 3, 0, 0)),
            pl.BlockSpec((1, 512, 512), lambda i: (i // 3, 0, 0)),
        ],
        out_specs=[rows, rows],
        out_shape=[shape, shape],
        compiler_params=pltpu.CompilerParams(vmem_limit_bytes=40 * 1024 * 1024),
        cost_estimate=pl.CostEstimate(flops=4_800_000_000, bytes_accessed=8_500_000, transcendentals=800_000),
    )(x.reshape(16, 80, 512), g.reshape(16, 80, 512), ups, downs)
    return back.reshape(32, PAIR, 512), out.reshape(32, PAIR, 512)


def three(x):
    high = x.astype(BF)
    mid = (x - high.astype(F32)).astype(BF)
    low = (x - high.astype(F32) - mid.astype(F32)).astype(BF)
    return high, mid, low


def named_in(routes):
    lanes = lax.broadcasted_iota(jnp.int32, (1,) * routes.ndim + (64,), routes.ndim)
    return routes[..., None] == lanes


def slot_code(named):
    rows = named.shape[-2]
    below = (
        lax.broadcasted_iota(jnp.int32, (rows, rows), 0)
        > lax.broadcasted_iota(jnp.int32, (rows, rows), 1)
    ).astype(BF)
    rank = jnp.einsum("ij,...je->...ie", below, named.astype(BF), preferred_element_type=F32)
    return jnp.where(named, rank, -1.0).astype(BF)


def slot_layout(q, at):
    q = (q + 32 * (at % 2)) % PAIR
    other = jnp.where(q < 2 * MAIN, q // MAIN, (q - 2 * MAIN) // (CAP - MAIN))
    place = jnp.where(q < 2 * MAIN, q % MAIN, MAIN + (q - 2 * MAIN) % (CAP - MAIN))
    return other, place


def shift_x(x, d):
    return lax.ppermute(x, "x", [(i, (i + d) % 4) for i in range(4)])


def take(x, i, axis):
    return lax.dynamic_index_in_dim(x, i, axis, keepdims=False)


def shards(tokens, routes, mix_weights, gate_up, down, w_in, grad_combined):
    rows = tokens.shape[0]
    gate_up, down = gate_up[0], down[0]
    core, at, plane = lax.axis_index("c"), lax.axis_index("x"), lax.axis_index("z")
    slots = 64 * CAP

    w_part = lax.all_to_all(
        jnp.broadcast_to(w_in[None], (64,) + w_in.shape), YZ, split_axis=0, concat_axis=0, tiled=True
    ).reshape(512, 512)

    payload = jnp.concatenate(
        [grad_combined, routes.astype(BF), *three(mix_weights), jnp.zeros((rows, 96), BF)], axis=1
    )
    column = lax.all_gather(payload, "z", axis=0, tiled=True).reshape(8, rows, 640)

    ordered = column_order(tokens)
    feats = ordered.reshape(rows, 4, 2, 512).transpose(2, 1, 0, 3)
    mine = take(feats, core, 0)
    theirs = swap_core(take(feats, 1 - core, 0))
    both = jnp.stack([jnp.where(core == 0, mine, theirs), jnp.where(core == 0, theirs, mine)], axis=1)
    blocks = [take(both, at, 0)]
    for d in (1, 2, 3):
        blocks.append(shift_x(take(both, (at + d) % 4, 0), d))
    blocks = jnp.stack(blocks)
    feature_block = jnp.stack([take(blocks, (at - j) % 4, 0) for j in range(4)])

    gate_up2, down2 = swap_core(gate_up), swap_core(down)
    ups = jnp.stack([gate_up, gate_up2])
    downs = jnp.stack([down, down2])

    partial = mm(feature_block.reshape(8 * rows, 512), w_part).astype(BF).reshape(8, rows, 512)
    partials = lax.all_to_all(partial, XC, split_axis=0, concat_axis=0, tiled=True)
    latent = jnp.sum(partials.astype(F32), axis=0).astype(BF)

    r = lax.broadcasted_iota(jnp.int32, (1, slots), 1)
    other, place = slot_layout(r % PAIR, at)
    spread = (
        lax.broadcasted_iota(jnp.int32, (64, slots), 0) == (r // PAIR) * 2 + (core + other) % 2
    ).astype(BF)
    code = slot_code(jnp.any(named_in(routes), axis=1))
    onehot = (mm(code, spread) == place.astype(F32)).astype(BF)
    out_send = mm(onehot, latent, ((0,), (0,))).astype(BF).reshape(32, PAIR, 512)
    recv = lax.all_to_all(out_send, ZX, split_axis=0, concat_axis=0, tiled=True)

    r = lax.broadcasted_iota(jnp.int32, (1, 4 * PAIR), 1)
    other, place = slot_layout(r % PAIR, at)
    spread = (
        lax.broadcasted_iota(jnp.int32, (64, 4 * PAIR), 0)
        == plane * 8 + (at + r // PAIR) % 4 * 2 + (core + other) % 2
    ).astype(BF)
    hit = named_in(column[:, :, 512:520].astype(jnp.int32))
    code = slot_code(jnp.any(hit, axis=2)).reshape(8 * rows, 64)
    send = (mm(code, spread) == place.astype(F32)).reshape(8, rows, 4 * PAIR)
    at_slot = 0.0
    for i in (1, 2, 3):
        piece = column[:, :, 512 + 8 * i : 520 + 8 * i].astype(F32)
        piece = jnp.sum(jnp.where(hit, piece[..., None], 0.0), axis=2).astype(BF)
        at_slot = at_slot + mm(piece.reshape(8 * rows, 64), spread)
    weight = jnp.where(send, at_slot.reshape(8, rows, 4 * PAIR), 0.0)
    picked = jnp.einsum(
        "ztr,ztl->zrl", send.astype(BF), column[:, :, :512], preferred_element_type=F32
    )
    grad_send = (jnp.sum(weight, axis=1)[..., None] * picked).astype(BF).reshape(8, 4, PAIR, 512)
    blocks = jnp.stack([grad_send[:, 0]] + [shift_x(grad_send[:, d], d) for d in (1, 2, 3)])
    grad_recv = jnp.stack([take(blocks, (at - j) % 4, 0) for j in range(4)], axis=1)

    grad_rows, outputs = expert_rows(recv, grad_recv, ups, downs)
    grad_back = lax.all_to_all(grad_rows, ZX, split_axis=0, concat_axis=0, tiled=True)

    out4 = outputs.reshape(8, 4, PAIR, 512)
    back = [take(out4, at, 1)] + [shift_x(take(out4, (at - d) % 4, 1), -d) for d in (1, 2, 3)]
    back = jnp.stack(back, axis=1).reshape(8, 4 * PAIR, 512)
    weight_hi = weight.astype(BF)
    weight_lo = (weight - weight_hi.astype(F32)).astype(BF)
    mixed = sum(
        jnp.einsum("ztr,zrl->ztl", w, back, preferred_element_type=F32) for w in (weight_hi, weight_lo)
    )
    combined = lax.psum_scatter(
        mixed.astype(BF).reshape(8 * rows, 512), "z", scatter_dimension=0, tiled=True
    )

    grad_latent = mm(onehot, grad_back.reshape(slots, 512)).astype(BF)
    line_grads = lax.all_gather(grad_latent, "x", axis=0, tiled=True)
    other_grads = swap_core(line_grads)
    tokens_mine = take(feature_block, core, 1).reshape(4 * rows, 512)
    tokens_other = take(feature_block, 1 - core, 1).reshape(4 * rows, 512)
    first = ((0,), (0,))
    part = mm(tokens_mine, line_grads, first) + mm(tokens_other, other_grads, first)
    part = part.astype(BF).reshape(64, 8, 512)
    parts = lax.all_to_all(part, YZ, split_axis=0, concat_axis=0, tiled=True)
    grad_w_in = jnp.sum(parts.astype(F32), axis=0) / rows

    w_all = lax.all_gather(after(w_part, recv), XC, axis=0, tiled=True)
    w_natural = w_all.reshape(8, 64, 8, 512).transpose(1, 0, 2, 3).reshape(4096, 512)
    grad_tokens = mm(grad_latent, w_natural, ((1,), (1,))).astype(BF)
    return combined, grad_tokens, grad_w_in


def solution(mesh):
    split = Mesh(mesh.devices.reshape(8, 8, 4, 2), ("dp", "z", "x", "c"))
    every = P(("dp", "z", "x", "c"), None)
    each = P(("z", "x", "c"), None, None)
    return jax.shard_map(
        shards,
        mesh=split,
        in_specs=(every, every, every, each, each, every, every),
        out_specs=(every, every, every),
        check_vma=False,
    )
```

```python
import jax
import jax.numpy as jnp
from jax import lax
from jax.experimental import pallas as pl
from jax.experimental.pallas import tpu as pltpu
from jax.sharding import Mesh, PartitionSpec as P

BF = jnp.bfloat16
F32 = jnp.float32
XC = ("x", "c")
YZ = ("dp", "z")
ZX = ("z", "x")
CAP = 20
MAIN = 16
PAIR = 2 * CAP


def mm(a, b, dims=((1,), (0,))):
    return lax.dot_general(a, b, (dims, ((), ())), preferred_element_type=F32)


def after(x, *deps):
    return lax.optimization_barrier((x,) + deps)[0]


def swap_core(x):
    return lax.ppermute(x, "c", [(0, 1), (1, 0)])


def column_target(core, at):
    a = lax.broadcasted_iota(jnp.int32, (1, 1024), 1)
    y, z, x, c, i = a // 512, (a // 64) % 8, (a // 16) % 4, (a // 8) % 2, a % 8
    d, m = (x - at) % 4, (c - core) % 2
    return (d * 2 + m) * 128 + y * 64 + z * 8 + i


def make_pick(to_ref, pick_ref):
    @pl.when(pl.program_id(0) == 0)
    def _():
        at = lax.broadcasted_iota(jnp.int32, (1024, 1024), 0)
        pick_ref[...] = jnp.where(to_ref[...] == at, 1.0, 0.0).astype(BF)


def split_kernel(to_ref, tokens_ref, mine_ref, theirs_ref, pick_ref):
    make_pick(to_ref, pick_ref)
    out = mm(tokens_ref[...], pick_ref[...], ((1,), (1,))).astype(BF)
    for d in range(4):
        mine_ref[d] = out[:, 256 * d : 256 * d + 128]
        theirs_ref[d] = out[:, 256 * d + 128 : 256 * d + 256]


def split_columns(to, tokens):
    rows = tokens.shape[0]
    shape = jax.ShapeDtypeStruct((4, rows, 512), BF)
    part = pl.BlockSpec((4, rows, 128), lambda p: (0, 0, p))
    return pl.pallas_call(
        split_kernel,
        grid=(4,),
        in_specs=[pl.BlockSpec((1, 1024), lambda p: (0, 0)), pl.BlockSpec((rows, 1024), lambda p: (0, p))],
        out_specs=[part, part],
        out_shape=[shape, shape],
        scratch_shapes=[pltpu.VMEM((1024, 1024), BF)],
        compiler_params=pltpu.CompilerParams(vmem_limit_bytes=32 * 1024 * 1024),
        cost_estimate=pl.CostEstimate(flops=1_100_000_000, bytes_accessed=2_100_000, transcendentals=0),
    )(to, tokens)


def join_kernel(to_ref, near_ref, far_ref, b1_ref, b2_ref, b3_ref, out_ref, pick_ref):
    make_pick(to_ref, pick_ref)
    parts = [near_ref[...], far_ref[...]]
    for ref in (b1_ref, b2_ref, b3_ref):
        parts += [ref[0], ref[1]]
    out_ref[...] = mm(jnp.concatenate(parts, axis=1), pick_ref[...]).astype(BF)


def join_columns(to, near, far, *others):
    rows = near.shape[0]
    one = pl.BlockSpec((rows, 128), lambda p: (0, p))
    two = pl.BlockSpec((2, rows, 128), lambda p: (0, 0, p))
    return pl.pallas_call(
        join_kernel,
        grid=(4,),
        in_specs=[pl.BlockSpec((1, 1024), lambda p: (0, 0)), one, one, two, two, two],
        out_specs=pl.BlockSpec((rows, 1024), lambda p: (0, p)),
        out_shape=jax.ShapeDtypeStruct((rows, 4096), BF),
        scratch_shapes=[pltpu.VMEM((1024, 1024), BF)],
        compiler_params=pltpu.CompilerParams(vmem_limit_bytes=32 * 1024 * 1024),
        cost_estimate=pl.CostEstimate(flops=1_100_000_000, bytes_accessed=2_100_000, transcendentals=0),
    )(to, near, far, *others)


def expert_kernel(x_ref, g_ref, up_ref, down_ref, back_ref, out_ref):
    w_up, w_down = up_ref[0], down_ref[0]
    x = x_ref[...].reshape(256, 512)
    g = g_ref[...].reshape(256, 512)
    pre = mm(x, w_up)
    grad_act = mm(g, w_down, ((1,), (1,)))
    gate, upper = pre[:, :512], pre[:, 512:]
    sigma = jax.nn.sigmoid(gate)
    soft = gate * sigma
    act = (soft * upper).astype(BF)
    grad_gate = (grad_act * upper * sigma * (1.0 + gate * (1.0 - sigma))).astype(BF)
    grad_up = (grad_act * soft).astype(BF)
    last = ((1,), (1,))
    back = mm(grad_gate, w_up[:, :512], last) + mm(grad_up, w_up[:, 512:], last)
    back = back.astype(BF).reshape(16, 16, 512)
    out = mm(act, w_down).astype(BF).reshape(16, 16, 512)
    step = pl.program_id(0)

    @pl.when(step != 3)
    def _():
        back_ref[...] = back
        out_ref[...] = out

    @pl.when(step == 3)
    def _():
        keep = (lax.broadcasted_iota(jnp.int32, (16, 16, 512), 1) % 8) < 4
        back_ref[...] = jnp.where(keep, back_ref[...].astype(F32), back.astype(F32)).astype(BF)
        out_ref[...] = jnp.where(keep, out_ref[...].astype(F32), out.astype(F32)).astype(BF)


def expert_rows(x, g, ups, downs):
    def block(i):
        return (0, jnp.where(i == 0, 0, jnp.where(i == 1, 3, jnp.where(i < 4, 2, jnp.where(i == 4, 1, 4)))), 0)

    rows = pl.BlockSpec((16, 16, 512), block)
    shape = pltpu.HBM((16, 80, 512), BF)
    hbm = lambda x: pltpu.with_memory_space_constraint(x, pltpu.HBM)
    back, out = pl.pallas_call(
        expert_kernel,
        grid=(6,),
        in_specs=[
            rows,
            rows,
            pl.BlockSpec((1, 512, 1024), lambda i: (i // 3, 0, 0)),
            pl.BlockSpec((1, 512, 512), lambda i: (i // 3, 0, 0)),
        ],
        out_specs=[rows, rows],
        out_shape=[shape, shape],
        compiler_params=pltpu.CompilerParams(vmem_limit_bytes=40 * 1024 * 1024),
        cost_estimate=pl.CostEstimate(flops=4_800_000_000, bytes_accessed=8_500_000, transcendentals=800_000),
    )(x.reshape(16, 80, 512), hbm(g.reshape(16, 80, 512)), hbm(ups), hbm(downs))
    return back.reshape(32, PAIR, 512), out.reshape(32, PAIR, 512)


def three(x):
    high = x.astype(BF)
    mid = (x - high.astype(F32)).astype(BF)
    low = (x - high.astype(F32) - mid.astype(F32)).astype(BF)
    return high, mid, low


def named_in(routes):
    lanes = lax.broadcasted_iota(jnp.int32, (1,) * routes.ndim + (64,), routes.ndim)
    return routes[..., None] == lanes


def slot_code(named):
    rows = named.shape[-2]
    below = (
        lax.broadcasted_iota(jnp.int32, (rows, rows), 0)
        > lax.broadcasted_iota(jnp.int32, (rows, rows), 1)
    ).astype(BF)
    rank = jnp.einsum("ij,...je->...ie", below, named.astype(BF), preferred_element_type=F32)
    return jnp.where(named, rank, -1.0).astype(BF)


def slot_layout(q, at):
    q = (q + 32 * (at % 2)) % PAIR
    other = jnp.where(q < 2 * MAIN, q // MAIN, (q - 2 * MAIN) // (CAP - MAIN))
    place = jnp.where(q < 2 * MAIN, q % MAIN, MAIN + (q - 2 * MAIN) % (CAP - MAIN))
    return other, place


def shift_x(x, d):
    return lax.ppermute(x, "x", [(i, (i + d) % 4) for i in range(4)])


def take(x, i, axis):
    return lax.dynamic_index_in_dim(x, i, axis, keepdims=False)


def shards(tokens, routes, mix_weights, gate_up, down, w_in, grad_combined):
    rows = tokens.shape[0]
    gate_up, down = gate_up[0], down[0]
    core, at, plane = lax.axis_index("c"), lax.axis_index("x"), lax.axis_index("z")
    slots = 64 * CAP

    w_part = lax.all_to_all(
        jnp.broadcast_to(w_in[None], (64,) + w_in.shape), YZ, split_axis=0, concat_axis=0, tiled=True
    ).reshape(512, 512)

    payload = jnp.concatenate(
        [grad_combined, routes.astype(BF), *three(mix_weights), jnp.zeros((rows, 96), BF)], axis=1
    )
    column = lax.all_gather(payload, "z", axis=0, tiled=True).reshape(8, rows, 640)

    to = column_target(core, at)
    mine, theirs = split_columns(to, tokens)
    theirs = swap_core(theirs)
    both = jnp.stack([jnp.where(core == 0, mine, theirs), jnp.where(core == 0, theirs, mine)], axis=1)
    blocks = jnp.stack([both[0]] + [shift_x(both[d], d) for d in (1, 2, 3)])
    feature_block = jnp.stack([take(blocks, (at - j) % 4, 0) for j in range(4)])
    tokens_mine = take(feature_block, core, 1).reshape(4 * rows, 512)
    tokens_other = take(feature_block, 1 - core, 1).reshape(4 * rows, 512)

    gate_up2, down2 = swap_core(gate_up), swap_core(down)
    ups = jnp.stack([gate_up, gate_up2])
    downs = jnp.stack([down, down2])

    partial = mm(feature_block.reshape(8 * rows, 512), w_part).astype(BF).reshape(8, rows, 512)
    partials = lax.all_to_all(partial, XC, split_axis=0, concat_axis=0, tiled=True)
    latent = jnp.sum(partials.astype(F32), axis=0).astype(BF)

    r = lax.broadcasted_iota(jnp.int32, (1, slots), 1)
    other, place = slot_layout(r % PAIR, at)
    spread = (
        lax.broadcasted_iota(jnp.int32, (64, slots), 0) == (r // PAIR) * 2 + (core + other) % 2
    ).astype(BF)
    code = slot_code(jnp.any(named_in(routes), axis=1))
    onehot = (mm(code, spread) == place.astype(F32)).astype(BF)
    out_send = mm(onehot, latent, ((0,), (0,))).astype(BF).reshape(32, PAIR, 512)
    out_send = after(out_send, column, ups, downs, tokens_mine, tokens_other)
    recv = lax.all_to_all(out_send, ZX, split_axis=0, concat_axis=0, tiled=True)

    r = lax.broadcasted_iota(jnp.int32, (1, 4 * PAIR), 1)
    other, place = slot_layout(r % PAIR, at)
    spread = (
        lax.broadcasted_iota(jnp.int32, (64, 4 * PAIR), 0)
        == plane * 8 + (at + r // PAIR) % 4 * 2 + (core + other) % 2
    ).astype(BF)
    hit = named_in(column[:, :, 512:520].astype(jnp.int32))
    code = slot_code(jnp.any(hit, axis=2)).reshape(8 * rows, 64)
    send = (mm(code, spread) == place.astype(F32)).reshape(8, rows, 4 * PAIR)
    at_slot = 0.0
    for i in (1, 2, 3):
        piece = column[:, :, 512 + 8 * i : 520 + 8 * i].astype(F32)
        piece = jnp.sum(jnp.where(hit, piece[..., None], 0.0), axis=2).astype(BF)
        at_slot = at_slot + mm(piece.reshape(8 * rows, 64), spread)
    weight = jnp.where(send, at_slot.reshape(8, rows, 4 * PAIR), 0.0)
    picked = jnp.einsum(
        "ztr,ztl->zrl", send.astype(BF), column[:, :, :512], preferred_element_type=F32
    )
    grad_send = (jnp.sum(weight, axis=1)[..., None] * picked).astype(BF).reshape(8, 4, PAIR, 512)
    sent = jnp.stack([grad_send[:, 0]] + [shift_x(grad_send[:, d], d) for d in (1, 2, 3)])
    grad_recv = jnp.stack([take(sent, (at - j) % 4, 0) for j in range(4)], axis=1)

    grad_rows, outputs = expert_rows(recv, grad_recv, ups, downs)
    grad_back = lax.all_to_all(grad_rows, ZX, split_axis=0, concat_axis=0, tiled=True)

    out4 = outputs.reshape(8, 4, PAIR, 512)
    back = [take(out4, at, 1)] + [shift_x(take(out4, (at - d) % 4, 1), -d) for d in (1, 2, 3)]
    back = jnp.stack(back, axis=1).reshape(8, 4 * PAIR, 512)
    weight_hi = weight.astype(BF)
    weight_lo = (weight - weight_hi.astype(F32)).astype(BF)
    mixed = sum(
        jnp.einsum("ztr,zrl->ztl", w, back, preferred_element_type=F32) for w in (weight_hi, weight_lo)
    )
    mixed = mixed.reshape(8 * rows, 512)
    combined = lax.psum_scatter(mixed, "z", scatter_dimension=0, tiled=True).astype(BF)

    grad_back = after(grad_back, mixed)

    grad_latent = mm(onehot, grad_back.reshape(slots, 512)).astype(BF)
    line_grads = lax.all_gather(grad_latent, "x", axis=0, tiled=True)
    other_grads = swap_core(line_grads)
    first = ((0,), (0,))
    part = mm(tokens_mine, line_grads, first) + mm(tokens_other, other_grads, first)
    part = part.astype(BF).reshape(64, 8, 512)
    parts = lax.all_to_all(part, YZ, split_axis=0, concat_axis=0, tiled=True)

    last = ((1,), (1,))
    near = mm(line_grads, w_part, last).astype(BF).reshape(4, rows, 512)
    far = swap_core(mm(other_grads, w_part, last).astype(BF).reshape(4, rows, 512))
    back = [take(near, at, 0), take(far, at, 0)]
    for d in (1, 2, 3):
        there = (at - d) % 4
        back.append(shift_x(jnp.stack([take(near, there, 0), take(far, there, 0)]), -d))
    back[0] = after(back[0], parts)
    grad_tokens = join_columns(to, *back)
    grad_w_in = jnp.sum(parts.astype(F32), axis=0) / rows
    return combined, grad_tokens, grad_w_in


def solution(mesh):
    split = Mesh(mesh.devices.reshape(8, 8, 4, 2), ("dp", "z", "x", "c"))
    every = P(("dp", "z", "x", "c"), None)
    each = P(("z", "x", "c"), None, None)
    return jax.shard_map(
        shards,
        mesh=split,
        in_specs=(every, every, every, each, each, every, every),
        out_specs=(every, every, every),
        check_vma=False,
    )
```

```python
import jax
import jax.numpy as jnp
from jax import lax
from jax.experimental import pallas as pl
from jax.experimental.pallas import tpu as pltpu
from jax.sharding import Mesh, PartitionSpec as P

BF = jnp.bfloat16
F32 = jnp.float32
XC = ("x", "c")
YZ = ("dp", "z")
ZX = ("z", "x")
CAP = 20
MAIN = 16
PAIR = 2 * CAP


def mm(a, b, dims=((1,), (0,))):
    return lax.dot_general(a, b, (dims, ((), ())), preferred_element_type=F32)


def after(x, *deps):
    return lax.optimization_barrier((x,) + deps)[0]


def swap_core(x):
    return lax.ppermute(x, "c", [(0, 1), (1, 0)])


def column_target(core, at):
    a = lax.broadcasted_iota(jnp.int32, (1, 1024), 1)
    y, z, x, c, i = a // 512, (a // 64) % 8, (a // 16) % 4, (a // 8) % 2, a % 8
    d, m = (x - at) % 4, (c - core) % 2
    return (d * 2 + m) * 128 + y * 64 + z * 8 + i


def make_pick(to_ref, pick_ref):
    @pl.when(pl.program_id(0) == 0)
    def _():
        at = lax.broadcasted_iota(jnp.int32, (1024, 1024), 0)
        pick_ref[...] = jnp.where(to_ref[...] == at, 1.0, 0.0).astype(BF)


def split_kernel(to_ref, tokens_ref, mine_ref, theirs_ref, pick_ref):
    make_pick(to_ref, pick_ref)
    out = mm(tokens_ref[...], pick_ref[...], ((1,), (1,))).astype(BF)
    for d in range(4):
        mine_ref[d] = out[:, 256 * d : 256 * d + 128]
        theirs_ref[d] = out[:, 256 * d + 128 : 256 * d + 256]


def split_columns(to, tokens):
    rows = tokens.shape[0]
    shape = jax.ShapeDtypeStruct((4, rows, 512), BF)
    part = pl.BlockSpec((4, rows, 128), lambda p: (0, 0, p))
    return pl.pallas_call(
        split_kernel,
        grid=(4,),
        in_specs=[pl.BlockSpec((1, 1024), lambda p: (0, 0)), pl.BlockSpec((rows, 1024), lambda p: (0, p))],
        out_specs=[part, part],
        out_shape=[shape, shape],
        scratch_shapes=[pltpu.VMEM((1024, 1024), BF)],
        compiler_params=pltpu.CompilerParams(vmem_limit_bytes=32 * 1024 * 1024),
        cost_estimate=pl.CostEstimate(flops=1_100_000_000, bytes_accessed=2_100_000, transcendentals=0),
    )(to, pltpu.with_memory_space_constraint(tokens, pltpu.HBM))


def join_kernel(to_ref, near_ref, far_ref, b1_ref, b2_ref, b3_ref, out_ref, pick_ref):
    make_pick(to_ref, pick_ref)
    parts = [near_ref[...], far_ref[...]]
    for ref in (b1_ref, b2_ref, b3_ref):
        parts += [ref[0], ref[1]]
    out_ref[...] = mm(jnp.concatenate(parts, axis=1), pick_ref[...]).astype(BF)


def join_columns(to, near, far, *others):
    rows = near.shape[0]
    one = pl.BlockSpec((rows, 128), lambda p: (0, p))
    two = pl.BlockSpec((2, rows, 128), lambda p: (0, 0, p))
    return pl.pallas_call(
        join_kernel,
        grid=(4,),
        in_specs=[pl.BlockSpec((1, 1024), lambda p: (0, 0)), one, one, two, two, two],
        out_specs=pl.BlockSpec((rows, 1024), lambda p: (0, p)),
        out_shape=jax.ShapeDtypeStruct((rows, 4096), BF),
        scratch_shapes=[pltpu.VMEM((1024, 1024), BF)],
        compiler_params=pltpu.CompilerParams(vmem_limit_bytes=32 * 1024 * 1024),
        cost_estimate=pl.CostEstimate(flops=6_000_000_000, bytes_accessed=18_000_000, transcendentals=0),
    )(to, near, far, *others)


def cotangent_kernel(
    expert_ref, place_ref, col_ref, s0_ref, s1_ref, s2_ref, s3_ref, hi_ref, mid_ref, wide_ref, fold_ref, before_ref
):
    @pl.when(pl.program_id(0) == 0)
    def _():
        row = lax.broadcasted_iota(jnp.int32, (2048, 128), 0)
        lane = lax.broadcasted_iota(jnp.int32, (2048, 128), 1)
        wide_ref[...] = jnp.where(lane == row // 64, 1.0, 0.0).astype(BF)
        lane = lax.broadcasted_iota(jnp.int32, (160, 512), 1) % 64
        fold_ref[...] = jnp.where(lane == expert_ref[...], 1.0, 0.0).astype(BF)
        u = lax.broadcasted_iota(jnp.int32, (512, 512), 0)
        t = lax.broadcasted_iota(jnp.int32, (512, 512), 1)
        same = jnp.logical_and(u // 128 == t // 128, u < t)
        before_ref[...] = jnp.where(same, 1.0, 0.0).astype(BF)

    col = col_ref[...].reshape(512, 640)
    spread = mm(wide_ref[...], col[:, 512:], ((1,), (1,)))
    row = lax.broadcasted_iota(jnp.int32, (512, 512), 0) % 64
    hit = spread[:512] == row.astype(F32)
    fold = fold_ref[...]
    named = mm(fold, jnp.where(hit, 1.0, 0.0).astype(BF))
    rank = mm(named.astype(BF), before_ref[...])
    send = jnp.logical_and(named > 0.5, rank == place_ref[...].astype(F32))
    parts = []
    for i in range(3):
        part = mm(fold, jnp.where(hit, spread[512 * (i + 1) : 512 * (i + 2)], 0.0).astype(BF))
        parts.append(jnp.where(send, part, 0.0).astype(BF))
    for j in range(4):
        one = [part[:, 128 * j : 128 * (j + 1)] for part in parts]
        hi_ref[j], mid_ref[j] = one[0], one[1]
        g = col[128 * j : 128 * (j + 1), :512]
        total = mm(jnp.concatenate(one, axis=1), jnp.concatenate([g, g, g], axis=0))
        for d, ref in enumerate((s0_ref, s1_ref, s2_ref, s3_ref)):
            ref[j] = total[PAIR * d : PAIR * (d + 1)].astype(BF)


def cotangent_rows(expert, place, column):
    rows = column.shape[1]
    step = lambda *shape: pl.BlockSpec((4,) + shape, lambda z: (z, 0, 0))
    const = pl.BlockSpec((160, 1), lambda z: (0, 0))
    sent = jax.ShapeDtypeStruct((8, PAIR, 512), BF)
    weight = jax.ShapeDtypeStruct((8, 160, rows), BF)
    return pl.pallas_call(
        cotangent_kernel,
        grid=(2,),
        in_specs=[const, const, step(rows, 640)],
        out_specs=[step(PAIR, 512)] * 4 + [step(160, rows)] * 2,
        out_shape=[sent] * 4 + [weight] * 2,
        scratch_shapes=[pltpu.VMEM((2048, 128), BF), pltpu.VMEM((160, 512), BF), pltpu.VMEM((512, 512), BF)],
        compiler_params=pltpu.CompilerParams(vmem_limit_bytes=32 * 1024 * 1024),
        cost_estimate=pl.CostEstimate(flops=1_000_000_000, bytes_accessed=3_000_000, transcendentals=0),
    )(expert, place, pltpu.with_memory_space_constraint(column, pltpu.HBM))


def expert_kernel(x_ref, g_ref, up1, down1, up2, down2, back_ref, out_ref, up_ref, down_ref, sems):
    step = pl.program_id(0)
    copies = [
        [
            pltpu.make_async_copy(up, up_ref.at[e], sems.at[e, 0]),
            pltpu.make_async_copy(down, down_ref.at[e], sems.at[e, 1]),
        ]
        for e, (up, down) in enumerate(((up1, down1), (up2, down2)))
    ]

    @pl.when(step == 0)
    def _():
        for copy in copies[0] + copies[1]:
            copy.start()
        for copy in copies[0]:
            copy.wait()

    @pl.when(step == 3)
    def _():
        for copy in copies[1]:
            copy.wait()

    w_up, w_down = up_ref[step // 3], down_ref[step // 3]
    x = x_ref[...].reshape(256, 512)
    g = g_ref[...].reshape(256, 512)
    pre = mm(x, w_up)
    grad_act = mm(g, w_down, ((1,), (1,)))
    gate, upper = pre[:, :512], pre[:, 512:]
    sigma = jax.nn.sigmoid(gate)
    soft = gate * sigma
    act = (soft * upper).astype(BF)
    grad_gate = (grad_act * upper * sigma * (1.0 + gate * (1.0 - sigma))).astype(BF)
    grad_up = (grad_act * soft).astype(BF)
    last = ((1,), (1,))
    back = mm(grad_gate, w_up[:, :512], last) + mm(grad_up, w_up[:, 512:], last)
    back = back.astype(BF).reshape(16, 16, 512)
    out = mm(act, w_down).astype(BF).reshape(16, 16, 512)

    @pl.when(step != 3)
    def _():
        back_ref[...] = back
        out_ref[...] = out

    @pl.when(step == 3)
    def _():
        keep = (lax.broadcasted_iota(jnp.int32, (16, 16, 512), 1) % 8) < 4
        back_ref[...] = jnp.where(keep, back_ref[...].astype(F32), back.astype(F32)).astype(BF)
        out_ref[...] = jnp.where(keep, out_ref[...].astype(F32), out.astype(F32)).astype(BF)


def expert_rows(x, g, *weights):
    def block(i):
        return (0, jnp.where(i == 0, 0, jnp.where(i == 1, 3, jnp.where(i < 4, 2, jnp.where(i == 4, 1, 4)))), 0)

    rows = pl.BlockSpec((16, 16, 512), block)
    shape = pltpu.HBM((16, 80, 512), BF)
    hbm = lambda x: pltpu.with_memory_space_constraint(x, pltpu.HBM)
    back, out = pl.pallas_call(
        expert_kernel,
        grid=(6,),
        in_specs=[
            rows,
            rows,
            *[pl.BlockSpec(memory_space=pl.ANY)] * 4,
        ],
        out_specs=[rows, rows],
        out_shape=[shape, shape],
        scratch_shapes=[
            pltpu.VMEM((2, 512, 1024), BF),
            pltpu.VMEM((2, 512, 512), BF),
            pltpu.SemaphoreType.DMA((2, 2)),
        ],
        compiler_params=pltpu.CompilerParams(vmem_limit_bytes=40 * 1024 * 1024),
        cost_estimate=pl.CostEstimate(flops=4_800_000_000, bytes_accessed=8_500_000, transcendentals=800_000),
    )(x.reshape(16, 80, 512), hbm(g.reshape(16, 80, 512)), *map(hbm, weights))
    return back.reshape(32, PAIR, 512), out.reshape(32, PAIR, 512)


def three(x):
    high = x.astype(BF)
    mid = (x - high.astype(F32)).astype(BF)
    low = (x - high.astype(F32) - mid.astype(F32)).astype(BF)
    return high, mid, low


def named_in(routes):
    lanes = lax.broadcasted_iota(jnp.int32, (1,) * routes.ndim + (64,), routes.ndim)
    return routes[..., None] == lanes


def slot_code(named):
    rows = named.shape[-2]
    below = (
        lax.broadcasted_iota(jnp.int32, (rows, rows), 0)
        > lax.broadcasted_iota(jnp.int32, (rows, rows), 1)
    ).astype(BF)
    rank = jnp.einsum("ij,...je->...ie", below, named.astype(BF), preferred_element_type=F32)
    return jnp.where(named, rank, -1.0).astype(BF)


def slot_layout(q, at):
    q = (q + 32 * (at % 2)) % PAIR
    other = jnp.where(q < 2 * MAIN, q // MAIN, (q - 2 * MAIN) // (CAP - MAIN))
    place = jnp.where(q < 2 * MAIN, q % MAIN, MAIN + (q - 2 * MAIN) % (CAP - MAIN))
    return other, place


def shift_x(x, d):
    return lax.ppermute(x, "x", [(i, (i + d) % 4) for i in range(4)])


def take(x, i, axis):
    return lax.dynamic_index_in_dim(x, i, axis, keepdims=False)


def shards(tokens, routes, mix_weights, gate_up, down, w_in, grad_combined):
    rows = tokens.shape[0]
    gate_up, down = gate_up[0], down[0]
    core, at, plane = lax.axis_index("c"), lax.axis_index("x"), lax.axis_index("z")
    slots = 64 * CAP

    w_part = lax.all_to_all(
        jnp.broadcast_to(w_in[None], (64,) + w_in.shape), YZ, split_axis=0, concat_axis=0, tiled=True
    ).reshape(512, 512)

    payload = jnp.concatenate(
        [grad_combined, routes.astype(BF), *three(mix_weights), jnp.zeros((rows, 96), BF)], axis=1
    )
    column = lax.all_gather(payload, "z", axis=0, tiled=True).reshape(8, rows, 640)

    to = column_target(core, at)
    mine, theirs = split_columns(to, tokens)
    theirs = swap_core(theirs)
    both = jnp.stack([jnp.where(core == 0, mine, theirs), jnp.where(core == 0, theirs, mine)], axis=1)
    blocks = jnp.stack([both[0]] + [shift_x(both[d], d) for d in (1, 2, 3)])
    feature_block = jnp.stack([take(blocks, (at - j) % 4, 0) for j in range(4)])
    tokens_mine = take(feature_block, core, 1).reshape(4 * rows, 512)
    tokens_other = take(feature_block, 1 - core, 1).reshape(4 * rows, 512)

    gate_up2, down2 = swap_core(after(gate_up, w_part)), swap_core(after(down, w_part))
    w_other = swap_core(w_part)

    partial = mm(feature_block.reshape(8 * rows, 512), w_part).astype(BF).reshape(8, rows, 512)
    partials = lax.all_to_all(partial, XC, split_axis=0, concat_axis=0, tiled=True)

    r = lax.broadcasted_iota(jnp.int32, (4 * PAIR, 1), 0)
    other, place = slot_layout(r % PAIR, at)
    expert = plane * 8 + (at + r // PAIR) % 4 * 2 + (core + other) % 2
    *grad_send, weight_hi, weight_mid = cotangent_rows(expert, place, column)
    partials = after(partials, *grad_send)
    latent = jnp.sum(partials.astype(F32), axis=0).astype(BF)

    r = lax.broadcasted_iota(jnp.int32, (1, slots), 1)
    other, place = slot_layout(r % PAIR, at)
    spread = (
        lax.broadcasted_iota(jnp.int32, (64, slots), 0) == (r // PAIR) * 2 + (core + other) % 2
    ).astype(BF)
    code = slot_code(jnp.any(named_in(routes), axis=1))
    onehot = (mm(code, spread) == place.astype(F32)).astype(BF)
    out_send = mm(onehot, latent, ((0,), (0,))).astype(BF).reshape(32, PAIR, 512)
    out_send = after(out_send, gate_up2, down2, tokens_mine, tokens_other, w_other)
    recv = lax.all_to_all(out_send, ZX, split_axis=0, concat_axis=0, tiled=True)

    sent = jnp.stack([grad_send[0]] + [shift_x(grad_send[d], d) for d in (1, 2, 3)])
    grad_recv = jnp.stack([take(sent, (at - j) % 4, 0) for j in range(4)], axis=1)

    grad_rows, outputs = expert_rows(recv, grad_recv, gate_up, down, gate_up2, down2)
    grad_back = lax.all_to_all(grad_rows, ZX, split_axis=0, concat_axis=0, tiled=True)

    out4 = outputs.reshape(8, 4, PAIR, 512)
    back = [take(out4, at, 1)] + [shift_x(take(out4, (at - d) % 4, 1), -d) for d in (1, 2, 3)]
    back = jnp.stack(back, axis=1).reshape(8, 4 * PAIR, 512)
    mixed = sum(
        jnp.einsum("zrt,zrl->ztl", w, back, preferred_element_type=F32) for w in (weight_hi, weight_mid)
    )
    mixed = mixed.reshape(8 * rows, 512)
    combined = lax.psum_scatter(mixed, "z", scatter_dimension=0, tiled=True).astype(BF)

    grad_back = after(grad_back, mixed)

    grad_latent = mm(onehot, grad_back.reshape(slots, 512)).astype(BF)
    line_grads = lax.all_gather(grad_latent, "x", axis=0, tiled=True)
    other_grads = swap_core(line_grads)
    first = ((0,), (0,))
    part = mm(tokens_mine, line_grads, first) + mm(tokens_other, other_grads, first)
    part = part.astype(BF).reshape(64, 8, 512)
    parts = lax.all_to_all(part, YZ, split_axis=0, concat_axis=0, tiled=True)

    last = ((1,), (1,))
    near = mm(line_grads, w_part, last).astype(BF).reshape(4, rows, 512)
    far = mm(line_grads, w_other, last).astype(BF).reshape(4, rows, 512)
    back = [take(near, at, 0), take(far, at, 0)]
    for d in (1, 2, 3):
        there = (at - d) % 4
        back.append(shift_x(jnp.stack([take(near, there, 0), take(far, there, 0)]), -d))
    back[0] = after(back[0], parts)
    grad_tokens = join_columns(to, *back)
    grad_w_in = jnp.sum(parts.astype(F32), axis=0) / rows
    return combined, grad_tokens, grad_w_in


def solution(mesh):
    split = Mesh(mesh.devices.reshape(8, 8, 4, 2), ("dp", "z", "x", "c"))
    every = P(("dp", "z", "x", "c"), None)
    each = P(("z", "x", "c"), None, None)
    return jax.shard_map(
        shards,
        mesh=split,
        in_specs=(every, every, every, each, each, every, every),
        out_specs=(every, every, every),
        check_vma=False,
    )
```

```python
import jax
import jax.numpy as jnp
from jax import lax
from jax.experimental import pallas as pl
from jax.experimental.pallas import tpu as pltpu
from jax.sharding import Mesh, PartitionSpec as P

BF = jnp.bfloat16
F32 = jnp.float32
XC = ("x", "c")
YZ = ("dp", "z")
ZX = ("z", "x")
CAP = 20
MAIN = 16
PAIR = 2 * CAP


def mm(a, b, dims=((1,), (0,))):
    return lax.dot_general(a, b, (dims, ((), ())), preferred_element_type=F32)


def after(x, *deps):
    return lax.optimization_barrier((x,) + deps)[0]


def swap_core(x):
    return lax.ppermute(x, "c", [(0, 1), (1, 0)])


def column_target(core, at):
    a = lax.broadcasted_iota(jnp.int32, (1, 1024), 1)
    y, z, x, c, i = a // 512, (a // 64) % 8, (a // 16) % 4, (a // 8) % 2, a % 8
    d, m = (x - at) % 4, (c - core) % 2
    return (d * 2 + m) * 128 + y * 64 + z * 8 + i


def make_pick(to_ref, pick_ref):
    @pl.when(pl.program_id(0) == 0)
    def _():
        at = lax.broadcasted_iota(jnp.int32, (1024, 1024), 0)
        pick_ref[...] = jnp.where(to_ref[...] == at, 1.0, 0.0).astype(BF)


def split_kernel(to_ref, tokens_ref, mine_ref, theirs_ref, pick_ref):
    make_pick(to_ref, pick_ref)
    out = mm(tokens_ref[...], pick_ref[...], ((1,), (1,))).astype(BF)
    for d in range(4):
        mine_ref[d] = out[:, 256 * d : 256 * d + 128]
        theirs_ref[d] = out[:, 256 * d + 128 : 256 * d + 256]


def split_columns(to, tokens):
    rows = tokens.shape[0]
    shape = jax.ShapeDtypeStruct((4, rows, 512), BF)
    part = pl.BlockSpec((4, rows, 128), lambda p: (0, 0, p))
    return pl.pallas_call(
        split_kernel,
        grid=(4,),
        in_specs=[pl.BlockSpec((1, 1024), lambda p: (0, 0)), pl.BlockSpec((rows, 1024), lambda p: (0, p))],
        out_specs=[part, part],
        out_shape=[shape, shape],
        scratch_shapes=[pltpu.VMEM((1024, 1024), BF)],
        compiler_params=pltpu.CompilerParams(vmem_limit_bytes=32 * 1024 * 1024),
        cost_estimate=pl.CostEstimate(flops=1_100_000_000, bytes_accessed=2_100_000, transcendentals=0),
    )(to, pltpu.with_memory_space_constraint(tokens, pltpu.HBM))


def join_kernel(to_ref, *refs):
    *parts, out_ref, pick_ref = refs
    make_pick(to_ref, pick_ref)
    out_ref[...] = mm(jnp.concatenate([ref[...] for ref in parts], axis=1), pick_ref[...]).astype(BF)


def join_columns(to, *slices):
    rows = slices[0].shape[0]
    near = pl.BlockSpec((rows, 128), lambda p: (0, p))
    far = pl.BlockSpec((rows, 128), lambda p: (0, p + 4))
    return pl.pallas_call(
        join_kernel,
        grid=(4,),
        in_specs=[pl.BlockSpec((1, 1024), lambda p: (0, 0))] + [near, far] * 4,
        out_specs=pl.BlockSpec((rows, 1024), lambda p: (0, p)),
        out_shape=jax.ShapeDtypeStruct((rows, 4096), BF),
        scratch_shapes=[pltpu.VMEM((1024, 1024), BF)],
        compiler_params=pltpu.CompilerParams(vmem_limit_bytes=32 * 1024 * 1024),
        cost_estimate=pl.CostEstimate(flops=9_000_000_000, bytes_accessed=28_000_000, transcendentals=0),
    )(to, *[x for pair in slices for x in (pair, pair)])


def cotangent_kernel(
    expert_ref, place_ref, col_ref, s0_ref, s1_ref, s2_ref, s3_ref, hi_ref, mid_ref, wide_ref, fold_ref, before_ref
):
    @pl.when(pl.program_id(0) == 0)
    def _():
        row = lax.broadcasted_iota(jnp.int32, (2048, 128), 0)
        lane = lax.broadcasted_iota(jnp.int32, (2048, 128), 1)
        wide_ref[...] = jnp.where(lane == row // 64, 1.0, 0.0).astype(BF)
        lane = lax.broadcasted_iota(jnp.int32, (160, 512), 1) % 64
        fold_ref[...] = jnp.where(lane == expert_ref[...], 1.0, 0.0).astype(BF)
        u = lax.broadcasted_iota(jnp.int32, (512, 512), 0)
        t = lax.broadcasted_iota(jnp.int32, (512, 512), 1)
        same = jnp.logical_and(u // 128 == t // 128, u < t)
        before_ref[...] = jnp.where(same, 1.0, 0.0).astype(BF)

    col = col_ref[...].reshape(512, 640)
    spread = mm(wide_ref[...], col[:, 512:], ((1,), (1,)))
    row = lax.broadcasted_iota(jnp.int32, (512, 512), 0) % 64
    hit = spread[:512] == row.astype(F32)
    fold = fold_ref[...]
    named = mm(fold, jnp.where(hit, 1.0, 0.0).astype(BF))
    rank = mm(named.astype(BF), before_ref[...])
    send = jnp.logical_and(named > 0.5, rank == place_ref[...].astype(F32))
    parts = []
    for i in range(3):
        part = mm(fold, jnp.where(hit, spread[512 * (i + 1) : 512 * (i + 2)], 0.0).astype(BF))
        parts.append(jnp.where(send, part, 0.0).astype(BF))
    for j in range(4):
        one = [part[:, 128 * j : 128 * (j + 1)] for part in parts]
        hi_ref[j], mid_ref[j] = one[0], one[1]
        g = col[128 * j : 128 * (j + 1), :512]
        total = mm(jnp.concatenate(one, axis=1), jnp.concatenate([g, g, g], axis=0))
        for d, ref in enumerate((s0_ref, s1_ref, s2_ref, s3_ref)):
            ref[j] = total[PAIR * d : PAIR * (d + 1)].astype(BF)


def cotangent_rows(expert, place, column):
    rows = column.shape[1]
    step = lambda *shape: pl.BlockSpec((4,) + shape, lambda z: (z, 0, 0))
    const = pl.BlockSpec((160, 1), lambda z: (0, 0))
    sent = jax.ShapeDtypeStruct((8, PAIR, 512), BF)
    weight = jax.ShapeDtypeStruct((8, 160, rows), BF)
    return pl.pallas_call(
        cotangent_kernel,
        grid=(2,),
        in_specs=[const, const, step(rows, 640)],
        out_specs=[step(PAIR, 512)] * 4 + [step(160, rows)] * 2,
        out_shape=[sent] * 4 + [weight] * 2,
        scratch_shapes=[pltpu.VMEM((2048, 128), BF), pltpu.VMEM((160, 512), BF), pltpu.VMEM((512, 512), BF)],
        compiler_params=pltpu.CompilerParams(vmem_limit_bytes=32 * 1024 * 1024),
        cost_estimate=pl.CostEstimate(flops=1_000_000_000, bytes_accessed=3_000_000, transcendentals=0),
    )(expert, place, pltpu.with_memory_space_constraint(column, pltpu.HBM))


ORDER = (0, 3, 2, 1, 4)


def expert_block(x, g, w_up, w_down):
    pre = mm(x, w_up)
    grad_act = mm(g, w_down, ((1,), (1,)))
    gate, upper = pre[:, :512], pre[:, 512:]
    sigma = jax.nn.sigmoid(gate)
    soft = gate * sigma
    act = (soft * upper).astype(BF)
    grad_gate = (grad_act * upper * sigma * (1.0 + gate * (1.0 - sigma))).astype(BF)
    grad_up = (grad_act * soft).astype(BF)
    back = mm(jnp.concatenate([grad_gate, grad_up], axis=1), w_up, ((1,), (1,)))
    return back, mm(act, w_down)


def start(*groups):
    for copies in groups:
        for copy in copies:
            copy.start()


def wait(copies):
    for copy in copies:
        copy.wait()


def expert_kernel(
    x_ref, g_ref, up1, down1, up2, down2, back_ref, out_ref,
    x_in, g_in, back_to, out_to, up_ref, down_ref, w_sems, in_sems, out_sems
):
    weights = [
        [
            pltpu.make_async_copy(up, up_ref.at[e], w_sems.at[e, 0]),
            pltpu.make_async_copy(down, down_ref.at[e], w_sems.at[e, 1]),
        ]
        for e, (up, down) in enumerate(((up1, down1), (up2, down2)))
    ]
    rows, sent = [], []
    for n, b in enumerate(ORDER):
        part = (slice(None), pl.ds(16 * b, 16))
        rows.append([
            pltpu.make_async_copy(x_ref.at[part], x_in.at[n], in_sems.at[n, 0]),
            pltpu.make_async_copy(g_ref.at[part], g_in.at[n], in_sems.at[n, 1]),
        ])
        sent.append([
            pltpu.make_async_copy(back_to.at[n], back_ref.at[part], out_sems.at[n, 0]),
            pltpu.make_async_copy(out_to.at[n], out_ref.at[part], out_sems.at[n, 1]),
        ])
    start(rows[0], weights[0])

    def step(e, n):
        return expert_block(
            x_in[n].reshape(256, 512), g_in[n].reshape(256, 512), up_ref[e], down_ref[e]
        )

    wait(weights[0])
    start(*rows[1:], weights[1])
    for n in (0, 1):
        wait(rows[n])
        back, out = step(0, n)
        back_to[n] = back.astype(BF).reshape(16, 16, 512)
        out_to[n] = out.astype(BF).reshape(16, 16, 512)
        start(sent[n])
    wait(rows[2])
    own_back, own_out = step(0, 2)
    wait(weights[1])
    back, out = step(1, 2)
    keep = (lax.broadcasted_iota(jnp.int32, (256, 512), 0) % 8) < 4
    back_to[2] = jnp.where(keep, own_back, back).astype(BF).reshape(16, 16, 512)
    out_to[2] = jnp.where(keep, own_out, out).astype(BF).reshape(16, 16, 512)
    start(sent[2])
    for n in (3, 4):
        wait(rows[n])
        back, out = step(1, n)
        back_to[n] = back.astype(BF).reshape(16, 16, 512)
        out_to[n] = out.astype(BF).reshape(16, 16, 512)
        start(sent[n])
    for copies in sent:
        wait(copies)


def expert_rows(x, g, *weights):
    shape = pltpu.HBM((16, 80, 512), BF)
    hbm = lambda x: pltpu.with_memory_space_constraint(x, pltpu.HBM)
    block = pltpu.VMEM((5, 16, 16, 512), BF)
    back, out = pl.pallas_call(
        expert_kernel,
        in_specs=[pl.BlockSpec(memory_space=pl.ANY)] * 6,
        out_specs=[pl.BlockSpec(memory_space=pl.ANY)] * 2,
        out_shape=[shape, shape],
        scratch_shapes=[
            block,
            block,
            block,
            block,
            pltpu.VMEM((2, 512, 1024), BF),
            pltpu.VMEM((2, 512, 512), BF),
            pltpu.SemaphoreType.DMA((2, 2)),
            pltpu.SemaphoreType.DMA((5, 2)),
            pltpu.SemaphoreType.DMA((5, 2)),
        ],
        compiler_params=pltpu.CompilerParams(vmem_limit_bytes=40 * 1024 * 1024),
        cost_estimate=pl.CostEstimate(flops=4_800_000_000, bytes_accessed=8_500_000, transcendentals=800_000),
    )(x.reshape(16, 80, 512), hbm(g.reshape(16, 80, 512)), *map(hbm, weights))
    return back.reshape(32, PAIR, 512), out.reshape(32, PAIR, 512)


def three(x):
    high = x.astype(BF)
    mid = (x - high.astype(F32)).astype(BF)
    low = (x - high.astype(F32) - mid.astype(F32)).astype(BF)
    return high, mid, low


def named_in(routes):
    lanes = lax.broadcasted_iota(jnp.int32, (1,) * routes.ndim + (64,), routes.ndim)
    return routes[..., None] == lanes


def slot_code(named):
    rows = named.shape[-2]
    below = (
        lax.broadcasted_iota(jnp.int32, (rows, rows), 0)
        > lax.broadcasted_iota(jnp.int32, (rows, rows), 1)
    ).astype(BF)
    rank = jnp.einsum("ij,...je->...ie", below, named.astype(BF), preferred_element_type=F32)
    return jnp.where(named, rank, -1.0).astype(BF)


def slot_layout(q, at):
    q = (q + 32 * (at % 2)) % PAIR
    other = jnp.where(q < 2 * MAIN, q // MAIN, (q - 2 * MAIN) // (CAP - MAIN))
    place = jnp.where(q < 2 * MAIN, q % MAIN, MAIN + (q - 2 * MAIN) % (CAP - MAIN))
    return other, place


def shift_x(x, d):
    return lax.ppermute(x, "x", [(i, (i + d) % 4) for i in range(4)])


def take(x, i, axis):
    return lax.dynamic_index_in_dim(x, i, axis, keepdims=False)


def shards(tokens, routes, mix_weights, gate_up, down, w_in, grad_combined):
    rows = tokens.shape[0]
    gate_up, down = gate_up[0], down[0]
    core, at, plane = lax.axis_index("c"), lax.axis_index("x"), lax.axis_index("z")
    slots = 64 * CAP

    w_part = lax.all_to_all(
        jnp.broadcast_to(w_in[None], (64,) + w_in.shape), YZ, split_axis=0, concat_axis=0, tiled=True
    ).reshape(512, 512)

    payload = jnp.concatenate(
        [grad_combined, routes.astype(BF), *three(mix_weights), jnp.zeros((rows, 96), BF)], axis=1
    )
    column = lax.all_gather(payload, "z", axis=0, tiled=True).reshape(8, rows, 640)

    to = column_target(core, at)
    mine, theirs = split_columns(to, tokens)
    theirs = swap_core(theirs)
    both = jnp.stack([jnp.where(core == 0, mine, theirs), jnp.where(core == 0, theirs, mine)], axis=1)
    blocks = jnp.stack([both[0]] + [shift_x(both[d], d) for d in (1, 2, 3)])
    feature_block = jnp.stack([take(blocks, (at - j) % 4, 0) for j in range(4)])
    tokens_mine = take(feature_block, core, 1).reshape(4 * rows, 512)
    tokens_other = take(feature_block, 1 - core, 1).reshape(4 * rows, 512)

    gate_up2, down2 = swap_core(after(gate_up, w_part)), swap_core(after(down, w_part))
    w_both = jnp.concatenate([w_part, swap_core(w_part)])

    partial = mm(feature_block.reshape(8 * rows, 512), w_part).astype(BF).reshape(8, rows, 512)
    partials = lax.all_to_all(partial, XC, split_axis=0, concat_axis=0, tiled=True)

    r = lax.broadcasted_iota(jnp.int32, (4 * PAIR, 1), 0)
    other, place = slot_layout(r % PAIR, at)
    expert = plane * 8 + (at + r // PAIR) % 4 * 2 + (core + other) % 2
    *grad_send, weight_hi, weight_mid = cotangent_rows(expert, place, column)
    partials = after(partials, *grad_send)
    latent = jnp.sum(partials.astype(F32), axis=0).astype(BF)

    r = lax.broadcasted_iota(jnp.int32, (1, slots), 1)
    other, place = slot_layout(r % PAIR, at)
    spread = (
        lax.broadcasted_iota(jnp.int32, (64, slots), 0) == (r // PAIR) * 2 + (core + other) % 2
    ).astype(BF)
    code = slot_code(jnp.any(named_in(routes), axis=1))
    onehot = (mm(code, spread) == place.astype(F32)).astype(BF)
    out_send = mm(onehot, latent, ((0,), (0,))).astype(BF).reshape(32, PAIR, 512)
    out_send, w_both, *_ = lax.optimization_barrier(
        (out_send, w_both, gate_up2, down2, tokens_mine, tokens_other)
    )
    recv = lax.all_to_all(out_send, ZX, split_axis=0, concat_axis=0, tiled=True)

    sent = jnp.stack([grad_send[0]] + [shift_x(grad_send[d], d) for d in (1, 2, 3)])
    grad_recv = jnp.stack([take(sent, (at - j) % 4, 0) for j in range(4)], axis=1)

    grad_rows, outputs = expert_rows(recv, grad_recv, gate_up, down, gate_up2, down2)
    grad_back = lax.all_to_all(grad_rows, ZX, split_axis=0, concat_axis=0, tiled=True)

    out4 = outputs.reshape(8, 4, PAIR, 512)
    back = [take(out4, at, 1)] + [shift_x(take(out4, (at - d) % 4, 1), -d) for d in (1, 2, 3)]
    back = jnp.stack(back, axis=1).reshape(8, 4 * PAIR, 512)
    mixed = sum(
        jnp.einsum("zrt,zrl->ztl", w, back, preferred_element_type=F32) for w in (weight_hi, weight_mid)
    )
    mixed = mixed.reshape(8 * rows, 512)
    combined = lax.psum_scatter(mixed, "z", scatter_dimension=0, tiled=True).astype(BF)

    grad_back = after(grad_back, mixed)

    grad_latent = mm(onehot, grad_back.reshape(slots, 512)).astype(BF)
    line_grads = lax.all_gather(grad_latent, "x", axis=0, tiled=True)
    other_grads = swap_core(line_grads)
    first = ((0,), (0,))
    part = mm(tokens_mine, line_grads, first) + mm(tokens_other, other_grads, first)
    part = part.astype(BF).reshape(64, 8, 512)

    slices = mm(line_grads, w_both, ((1,), (1,))).astype(BF).reshape(4, rows, 1024)
    part = after(part, slices)
    parts = lax.all_to_all(part, YZ, split_axis=0, concat_axis=0, tiled=True)
    back = [take(slices, at, 0)] + [shift_x(take(slices, (at - d) % 4, 0), -d) for d in (1, 2, 3)]
    back[0] = after(back[0], parts)
    grad_tokens = join_columns(to, *back)
    grad_w_in = jnp.sum(parts.astype(F32), axis=0) / rows
    return combined, grad_tokens, grad_w_in


def solution(mesh):
    split = Mesh(mesh.devices.reshape(8, 8, 4, 2), ("dp", "z", "x", "c"))
    every = P(("dp", "z", "x", "c"), None)
    each = P(("z", "x", "c"), None, None)
    return jax.shard_map(
        shards,
        mesh=split,
        in_specs=(every, every, every, each, each, every, every),
        out_specs=(every, every, every),
        check_vma=False,
    )
```

```python
import jax
import jax.numpy as jnp
from jax import lax
from jax.experimental import pallas as pl
from jax.experimental.pallas import tpu as pltpu
from jax.sharding import Mesh, PartitionSpec as P

BF = jnp.bfloat16
F32 = jnp.float32
XC = ("x", "c")
YZ = ("dp", "z")
ZX = ("z", "x")
CAP = 20
MAIN = 16
PAIR = 2 * CAP


def mm(a, b, dims=((1,), (0,))):
    return lax.dot_general(a, b, (dims, ((), ())), preferred_element_type=F32)


def after(x, *deps):
    return lax.optimization_barrier((x,) + deps)[0]


def swap_core(x):
    return lax.ppermute(x, "c", [(0, 1), (1, 0)])


def column_target(core, at):
    a = lax.broadcasted_iota(jnp.int32, (1, 1024), 1)
    y, z, x, c, i = a // 512, (a // 64) % 8, (a // 16) % 4, (a // 8) % 2, a % 8
    d, m = (x - at) % 4, (c - core) % 2
    return (d * 2 + m) * 128 + y * 64 + z * 8 + i


def make_pick(to_ref, pick_ref):
    @pl.when(pl.program_id(0) == 0)
    def _():
        at = lax.broadcasted_iota(jnp.int32, (1024, 1024), 0)
        pick_ref[...] = jnp.where(to_ref[...] == at, 1.0, 0.0).astype(BF)


def split_kernel(to_ref, tokens_ref, mine_ref, theirs_ref, pick_ref):
    at = lax.broadcasted_iota(jnp.int32, (1024, 1024), 0)
    pick_ref[...] = jnp.where(to_ref[...] == at, 1.0, 0.0).astype(BF)
    tokens = jnp.concatenate([tokens_ref[:, 1024 * p : 1024 * (p + 1)] for p in range(4)], axis=0)
    out = mm(tokens, pick_ref[...], ((1,), (1,))).astype(BF)
    for p in range(4):
        for d in range(4):
            part = out[128 * p : 128 * (p + 1), 256 * d : 256 * (d + 1)]
            mine_ref[d, :, 128 * p : 128 * (p + 1)] = part[:, :128]
            theirs_ref[d, :, 128 * p : 128 * (p + 1)] = part[:, 128:]


def split_columns(to, tokens):
    rows = tokens.shape[0]
    shape = jax.ShapeDtypeStruct((4, rows, 512), BF)
    part = pl.BlockSpec((4, rows, 512), lambda p: (0, 0, 0))
    return pl.pallas_call(
        split_kernel,
        grid=(1,),
        in_specs=[pl.BlockSpec((1, 1024), lambda p: (0, 0)), pl.BlockSpec((rows, 4096), lambda p: (0, 0))],
        out_specs=[part, part],
        out_shape=[shape, shape],
        scratch_shapes=[pltpu.VMEM((1024, 1024), BF)],
        compiler_params=pltpu.CompilerParams(vmem_limit_bytes=32 * 1024 * 1024),
        cost_estimate=pl.CostEstimate(flops=1_100_000_000, bytes_accessed=2_100_000, transcendentals=0),
    )(to, pltpu.with_memory_space_constraint(tokens, pltpu.HBM))


def join_kernel(to_ref, *refs):
    *parts, out_ref, pick_ref = refs
    make_pick(to_ref, pick_ref)
    out_ref[...] = mm(jnp.concatenate([ref[...] for ref in parts], axis=1), pick_ref[...]).astype(BF)


def join_columns(to, *slices):
    rows = slices[0].shape[0]
    near = pl.BlockSpec((rows, 128), lambda p: (0, p))
    far = pl.BlockSpec((rows, 128), lambda p: (0, p + 4))
    return pl.pallas_call(
        join_kernel,
        grid=(4,),
        in_specs=[pl.BlockSpec((1, 1024), lambda p: (0, 0))] + [near, far] * 4,
        out_specs=pl.BlockSpec((rows, 1024), lambda p: (0, p)),
        out_shape=jax.ShapeDtypeStruct((rows, 4096), BF),
        scratch_shapes=[pltpu.VMEM((1024, 1024), BF)],
        compiler_params=pltpu.CompilerParams(vmem_limit_bytes=32 * 1024 * 1024),
        cost_estimate=pl.CostEstimate(flops=9_000_000_000, bytes_accessed=28_000_000, transcendentals=0),
    )(to, *[x for pair in slices for x in (pair, pair)])


def cotangent_kernel(
    expert_ref, place_ref, col_ref, s0_ref, s1_ref, s2_ref, s3_ref, hi_ref, mid_ref, wide_ref, fold_ref, before_ref
):
    @pl.when(pl.program_id(0) == 0)
    def _():
        row = lax.broadcasted_iota(jnp.int32, (2048, 128), 0)
        lane = lax.broadcasted_iota(jnp.int32, (2048, 128), 1)
        wide_ref[...] = jnp.where(lane == row // 64, 1.0, 0.0).astype(BF)
        lane = lax.broadcasted_iota(jnp.int32, (160, 512), 1) % 64
        fold_ref[...] = jnp.where(lane == expert_ref[...], 1.0, 0.0).astype(BF)
        u = lax.broadcasted_iota(jnp.int32, (512, 512), 0)
        t = lax.broadcasted_iota(jnp.int32, (512, 512), 1)
        same = jnp.logical_and(u // 128 == t // 128, u < t)
        before_ref[...] = jnp.where(same, 1.0, 0.0).astype(BF)

    col = col_ref[...].reshape(512, 640)
    spread = mm(wide_ref[...], col[:, 512:], ((1,), (1,)))
    row = lax.broadcasted_iota(jnp.int32, (512, 512), 0) % 64
    hit = spread[:512] == row.astype(F32)
    fold = fold_ref[...]
    named = mm(fold, jnp.where(hit, 1.0, 0.0).astype(BF))
    rank = mm(named.astype(BF), before_ref[...])
    send = jnp.logical_and(named > 0.5, rank == place_ref[...].astype(F32))
    parts = []
    for i in range(3):
        part = mm(fold, jnp.where(hit, spread[512 * (i + 1) : 512 * (i + 2)], 0.0).astype(BF))
        parts.append(jnp.where(send, part, 0.0).astype(BF))
    for j in range(4):
        one = [part[:, 128 * j : 128 * (j + 1)] for part in parts]
        hi_ref[j], mid_ref[j] = one[0], one[1]
        g = col[128 * j : 128 * (j + 1), :512]
        total = mm(jnp.concatenate(one, axis=1), jnp.concatenate([g, g, g], axis=0))
        for d, ref in enumerate((s0_ref, s1_ref, s2_ref, s3_ref)):
            ref[j] = total[PAIR * d : PAIR * (d + 1)].astype(BF)


def cotangent_rows(expert, place, column):
    rows = column.shape[1]
    step = lambda *shape: pl.BlockSpec((4,) + shape, lambda z: (z, 0, 0))
    const = pl.BlockSpec((160, 1), lambda z: (0, 0))
    sent = jax.ShapeDtypeStruct((8, PAIR, 512), BF)
    weight = jax.ShapeDtypeStruct((8, 160, rows), BF)
    return pl.pallas_call(
        cotangent_kernel,
        grid=(2,),
        in_specs=[const, const, step(rows, 640)],
        out_specs=[step(PAIR, 512)] * 4 + [step(160, rows)] * 2,
        out_shape=[sent] * 4 + [weight] * 2,
        scratch_shapes=[pltpu.VMEM((2048, 128), BF), pltpu.VMEM((160, 512), BF), pltpu.VMEM((512, 512), BF)],
        compiler_params=pltpu.CompilerParams(vmem_limit_bytes=32 * 1024 * 1024),
        cost_estimate=pl.CostEstimate(flops=1_000_000_000, bytes_accessed=3_000_000, transcendentals=0),
    )(expert, place, pltpu.with_memory_space_constraint(column, pltpu.HBM))


ORDER = (0, 3, 2, 1, 4)


def expert_block(x, g, w_up, w_down):
    pre = mm(x, w_up)
    grad_act = mm(g, w_down, ((1,), (1,)))
    gate, upper = pre[:, :512], pre[:, 512:]
    sigma = jax.nn.sigmoid(gate)
    soft = gate * sigma
    act = (soft * upper).astype(BF)
    grad_gate = (grad_act * upper * sigma * (1.0 + gate * (1.0 - sigma))).astype(BF)
    grad_up = (grad_act * soft).astype(BF)
    back = mm(jnp.concatenate([grad_gate, grad_up], axis=1), w_up, ((1,), (1,)))
    return back, mm(act, w_down)


def start(*groups):
    for copies in groups:
        for copy in copies:
            copy.start()


def wait(copies):
    for copy in copies:
        copy.wait()


def expert_kernel(
    x_ref, g_ref, up1, down1, up2, down2, back_ref, out_ref,
    x_in, g_in, back_to, out_to, up_ref, down_ref, w_sems, in_sems, out_sems
):
    weights = [
        [
            pltpu.make_async_copy(up, up_ref.at[e], w_sems.at[e, 0]),
            pltpu.make_async_copy(down, down_ref.at[e], w_sems.at[e, 1]),
        ]
        for e, (up, down) in enumerate(((up1, down1), (up2, down2)))
    ]
    rows, sent = [], []
    for n, b in enumerate(ORDER):
        part = (slice(None), pl.ds(16 * b, 16))
        rows.append([
            pltpu.make_async_copy(x_ref.at[part], x_in.at[n], in_sems.at[n, 0]),
            pltpu.make_async_copy(g_ref.at[part], g_in.at[n], in_sems.at[n, 1]),
        ])
        sent.append([
            pltpu.make_async_copy(back_to.at[n], back_ref.at[part], out_sems.at[n, 0]),
            pltpu.make_async_copy(out_to.at[n], out_ref.at[part], out_sems.at[n, 1]),
        ])
    start(rows[0], weights[0])

    def step(e, n):
        return expert_block(
            x_in[n].reshape(256, 512), g_in[n].reshape(256, 512), up_ref[e], down_ref[e]
        )

    wait(weights[0])
    start(*rows[1:], weights[1])
    for n in (0, 1):
        wait(rows[n])
        back, out = step(0, n)
        back_to[n] = back.astype(BF).reshape(16, 16, 512)
        out_to[n] = out.astype(BF).reshape(16, 16, 512)
        start(sent[n])
    wait(rows[2])
    own_back, own_out = step(0, 2)
    wait(weights[1])
    back, out = step(1, 2)
    keep = (lax.broadcasted_iota(jnp.int32, (256, 512), 0) % 8) < 4
    back_to[2] = jnp.where(keep, own_back, back).astype(BF).reshape(16, 16, 512)
    out_to[2] = jnp.where(keep, own_out, out).astype(BF).reshape(16, 16, 512)
    start(sent[2])
    for n in (3, 4):
        wait(rows[n])
        back, out = step(1, n)
        back_to[n] = back.astype(BF).reshape(16, 16, 512)
        out_to[n] = out.astype(BF).reshape(16, 16, 512)
        start(sent[n])
    for copies in sent:
        wait(copies)


def expert_rows(x, g, *weights):
    shape = pltpu.HBM((16, 80, 512), BF)
    hbm = lambda x: pltpu.with_memory_space_constraint(x, pltpu.HBM)
    block = pltpu.VMEM((5, 16, 16, 512), BF)
    back, out = pl.pallas_call(
        expert_kernel,
        in_specs=[pl.BlockSpec(memory_space=pl.ANY)] * 6,
        out_specs=[pl.BlockSpec(memory_space=pl.ANY)] * 2,
        out_shape=[shape, shape],
        scratch_shapes=[
            block,
            block,
            block,
            block,
            pltpu.VMEM((2, 512, 1024), BF),
            pltpu.VMEM((2, 512, 512), BF),
            pltpu.SemaphoreType.DMA((2, 2)),
            pltpu.SemaphoreType.DMA((5, 2)),
            pltpu.SemaphoreType.DMA((5, 2)),
        ],
        compiler_params=pltpu.CompilerParams(vmem_limit_bytes=40 * 1024 * 1024),
        cost_estimate=pl.CostEstimate(flops=4_800_000_000, bytes_accessed=8_500_000, transcendentals=800_000),
    )(x.reshape(16, 80, 512), hbm(g.reshape(16, 80, 512)), *map(hbm, weights))
    return back.reshape(32, PAIR, 512), out.reshape(32, PAIR, 512)


def three(x):
    high = x.astype(BF)
    mid = (x - high.astype(F32)).astype(BF)
    low = (x - high.astype(F32) - mid.astype(F32)).astype(BF)
    return high, mid, low


def named_in(routes):
    lanes = lax.broadcasted_iota(jnp.int32, (1,) * routes.ndim + (64,), routes.ndim)
    return routes[..., None] == lanes


def slot_code(named):
    rows = named.shape[-2]
    below = (
        lax.broadcasted_iota(jnp.int32, (rows, rows), 0)
        > lax.broadcasted_iota(jnp.int32, (rows, rows), 1)
    ).astype(BF)
    rank = jnp.einsum("ij,...je->...ie", below, named.astype(BF), preferred_element_type=F32)
    return jnp.where(named, rank, -1.0).astype(BF)


def slot_layout(q, at):
    q = (q + 32 * (at % 2)) % PAIR
    other = jnp.where(q < 2 * MAIN, q // MAIN, (q - 2 * MAIN) // (CAP - MAIN))
    place = jnp.where(q < 2 * MAIN, q % MAIN, MAIN + (q - 2 * MAIN) % (CAP - MAIN))
    return other, place


def shift_x(x, d):
    return lax.ppermute(x, "x", [(i, (i + d) % 4) for i in range(4)])


def take(x, i, axis):
    return lax.dynamic_index_in_dim(x, i, axis, keepdims=False)


def shards(tokens, routes, mix_weights, gate_up, down, w_in, grad_combined):
    rows = tokens.shape[0]
    gate_up, down = gate_up[0], down[0]
    core, at, plane = lax.axis_index("c"), lax.axis_index("x"), lax.axis_index("z")
    slots = 64 * CAP

    w_part = lax.all_to_all(
        jnp.broadcast_to(w_in[None], (64,) + w_in.shape), YZ, split_axis=0, concat_axis=0, tiled=True
    ).reshape(512, 512)

    payload = jnp.concatenate(
        [grad_combined, routes.astype(BF), *three(mix_weights), jnp.zeros((rows, 96), BF)], axis=1
    )
    column = lax.all_gather(payload, "z", axis=0, tiled=True).reshape(8, rows, 640)

    to = column_target(core, at)
    mine, theirs = split_columns(to, tokens)
    theirs = swap_core(theirs)
    both = jnp.stack([jnp.where(core == 0, mine, theirs), jnp.where(core == 0, theirs, mine)], axis=1)
    blocks = jnp.stack([both[0]] + [shift_x(both[d], d) for d in (1, 2, 3)])
    feature_block = jnp.stack([take(blocks, (at - j) % 4, 0) for j in range(4)])
    tokens_mine = take(feature_block, core, 1).reshape(4 * rows, 512)
    tokens_other = take(feature_block, 1 - core, 1).reshape(4 * rows, 512)

    gate_up2, down2 = swap_core(after(gate_up, w_part)), swap_core(after(down, w_part))
    w_both = jnp.concatenate([w_part, swap_core(w_part)])

    partial = mm(feature_block.reshape(8 * rows, 512), w_part).astype(BF).reshape(8, rows, 512)
    partials = lax.all_to_all(partial, XC, split_axis=0, concat_axis=0, tiled=True)

    r = lax.broadcasted_iota(jnp.int32, (4 * PAIR, 1), 0)
    other, place = slot_layout(r % PAIR, at)
    expert = plane * 8 + (at + r // PAIR) % 4 * 2 + (core + other) % 2
    *grad_send, weight_hi, weight_mid = cotangent_rows(expert, place, column)
    partials = after(partials, *grad_send)
    latent = jnp.sum(partials.astype(F32), axis=0).astype(BF)

    r = lax.broadcasted_iota(jnp.int32, (1, slots), 1)
    other, place = slot_layout(r % PAIR, at)
    spread = (
        lax.broadcasted_iota(jnp.int32, (64, slots), 0) == (r // PAIR) * 2 + (core + other) % 2
    ).astype(BF)
    code = slot_code(jnp.any(named_in(routes), axis=1))
    onehot = (mm(code, spread) == place.astype(F32)).astype(BF)
    out_send = mm(onehot, latent, ((0,), (0,))).astype(BF).reshape(32, PAIR, 512)
    out_send, w_both, *_ = lax.optimization_barrier(
        (out_send, w_both, gate_up2, down2, tokens_mine, tokens_other)
    )
    recv = lax.all_to_all(out_send, ZX, split_axis=0, concat_axis=0, tiled=True)

    sent = jnp.stack([grad_send[0]] + [shift_x(grad_send[d], d) for d in (1, 2, 3)])
    grad_recv = jnp.stack([take(sent, (at - j) % 4, 0) for j in range(4)], axis=1)

    grad_rows, outputs = expert_rows(recv, grad_recv, gate_up, down, gate_up2, down2)
    grad_back = lax.all_to_all(grad_rows, ZX, split_axis=0, concat_axis=0, tiled=True)

    out4 = outputs.reshape(8, 4, PAIR, 512)
    back = [take(out4, at, 1)] + [shift_x(take(out4, (at - d) % 4, 1), -d) for d in (1, 2, 3)]
    back = jnp.stack(back, axis=1).reshape(8, 4 * PAIR, 512)
    mixed = sum(
        jnp.einsum("zrt,zrl->ztl", w, back, preferred_element_type=F32) for w in (weight_hi, weight_mid)
    )
    mixed = mixed.reshape(8 * rows, 512)
    combined = lax.psum_scatter(mixed, "z", scatter_dimension=0, tiled=True).astype(BF)

    grad_back = after(grad_back, mixed)

    grad_latent = mm(onehot, grad_back.reshape(slots, 512)).astype(BF)
    line_grads = lax.all_gather(grad_latent, "x", axis=0, tiled=True)
    other_grads = swap_core(line_grads)
    first = ((0,), (0,))
    part = mm(tokens_mine, line_grads, first) + mm(tokens_other, other_grads, first)
    part = part.astype(BF).reshape(64, 8, 512)

    slices = mm(line_grads, w_both, ((1,), (1,))).astype(BF).reshape(4, rows, 1024)
    part = after(part, slices)
    parts = lax.all_to_all(part, YZ, split_axis=0, concat_axis=0, tiled=True)
    back = [take(slices, at, 0)] + [shift_x(take(slices, (at - d) % 4, 0), -d) for d in (1, 2, 3)]
    back[0] = after(back[0], parts)
    grad_tokens = join_columns(to, *back)
    grad_w_in = jnp.sum(parts.astype(F32), axis=0) / rows
    return combined, grad_tokens, grad_w_in


def solution(mesh):
    split = Mesh(mesh.devices.reshape(8, 8, 4, 2), ("dp", "z", "x", "c"))
    every = P(("dp", "z", "x", "c"), None)
    each = P(("z", "x", "c"), None, None)
    return jax.shard_map(
        shards,
        mesh=split,
        in_specs=(every, every, every, each, each, every, every),
        out_specs=(every, every, every),
        check_vma=False,
    )
```

```python
import jax
import jax.numpy as jnp
from jax import lax
from jax.experimental import pallas as pl
from jax.experimental.pallas import tpu as pltpu
from jax.sharding import Mesh, PartitionSpec as P

BF = jnp.bfloat16
F32 = jnp.float32
XC = ("x", "c")
YZ = ("dp", "z")
ZX = ("z", "x")
CAP = 20
MAIN = 16
PAIR = 2 * CAP


def mm(a, b, dims=((1,), (0,))):
    return lax.dot_general(a, b, (dims, ((), ())), preferred_element_type=F32)


def after(x, *deps):
    return lax.optimization_barrier((x,) + deps)[0]


def swap_core(x):
    return lax.ppermute(x, "c", [(0, 1), (1, 0)])


def column_target(core, at):
    a = lax.broadcasted_iota(jnp.int32, (1, 1024), 1)
    y, z, x, c, i = a // 512, (a // 64) % 8, (a // 16) % 4, (a // 8) % 2, a % 8
    d, m = (x - at) % 4, (c - core) % 2
    return (d * 2 + m) * 128 + y * 64 + z * 8 + i


def split_kernel(to_ref, tokens_ref, mine_ref, theirs_ref, pick_ref):
    at = lax.broadcasted_iota(jnp.int32, (1024, 1024), 0)
    pick_ref[...] = jnp.where(to_ref[...] == at, 1.0, 0.0).astype(BF)
    tokens = jnp.concatenate([tokens_ref[:, 1024 * p : 1024 * (p + 1)] for p in range(4)], axis=0)
    out = mm(tokens, pick_ref[...], ((1,), (1,))).astype(BF)
    for p in range(4):
        for d in range(4):
            part = out[128 * p : 128 * (p + 1), 256 * d : 256 * (d + 1)]
            mine_ref[d, :, 128 * p : 128 * (p + 1)] = part[:, :128]
            theirs_ref[d, :, 128 * p : 128 * (p + 1)] = part[:, 128:]


def split_columns(to, tokens):
    rows = tokens.shape[0]
    shape = jax.ShapeDtypeStruct((4, rows, 512), BF)
    part = pl.BlockSpec((4, rows, 512), lambda p: (0, 0, 0))
    return pl.pallas_call(
        split_kernel,
        grid=(1,),
        in_specs=[pl.BlockSpec((1, 1024), lambda p: (0, 0)), pl.BlockSpec((rows, 4096), lambda p: (0, 0))],
        out_specs=[part, part],
        out_shape=[shape, shape],
        scratch_shapes=[pltpu.VMEM((1024, 1024), BF)],
        compiler_params=pltpu.CompilerParams(vmem_limit_bytes=32 * 1024 * 1024),
        cost_estimate=pl.CostEstimate(flops=1_100_000_000, bytes_accessed=2_100_000, transcendentals=0),
    )(to, pltpu.with_memory_space_constraint(tokens, pltpu.HBM))


def join_kernel(to_ref, *refs):
    *slices, out_ref, pick_ref = refs
    at = lax.broadcasted_iota(jnp.int32, (1024, 1024), 0)
    pick_ref[...] = jnp.where(to_ref[...] == at, 1.0, 0.0).astype(BF)
    rows = []
    for p in range(4):
        cols = [ref[:, k + 128 * p : k + 128 * (p + 1)] for ref in slices for k in (0, 512)]
        rows.append(jnp.concatenate(cols, axis=1))
    out = mm(jnp.concatenate(rows, axis=0), pick_ref[...]).astype(BF)
    for p in range(4):
        out_ref[:, 1024 * p : 1024 * (p + 1)] = out[128 * p : 128 * (p + 1)]


def join_columns(to, *slices):
    rows = slices[0].shape[0]
    full = pl.BlockSpec((rows, 1024), lambda p: (0, 0))
    return pl.pallas_call(
        join_kernel,
        grid=(1,),
        in_specs=[pl.BlockSpec((1, 1024), lambda p: (0, 0))] + [full] * 4,
        out_specs=pl.BlockSpec((rows, 4096), lambda p: (0, 0)),
        out_shape=jax.ShapeDtypeStruct((rows, 4096), BF),
        scratch_shapes=[pltpu.VMEM((1024, 1024), BF)],
        compiler_params=pltpu.CompilerParams(vmem_limit_bytes=32 * 1024 * 1024),
        cost_estimate=pl.CostEstimate(flops=9_000_000_000, bytes_accessed=28_000_000, transcendentals=0),
    )(to, *slices)


def cotangent_kernel(
    expert_ref, place_ref, col_ref, s0_ref, s1_ref, s2_ref, s3_ref, hi_ref, mid_ref, wide_ref, fold_ref, before_ref
):
    @pl.when(pl.program_id(0) == 0)
    def _():
        row = lax.broadcasted_iota(jnp.int32, (2048, 128), 0)
        lane = lax.broadcasted_iota(jnp.int32, (2048, 128), 1)
        wide_ref[...] = jnp.where(lane == row // 64, 1.0, 0.0).astype(BF)
        lane = lax.broadcasted_iota(jnp.int32, (160, 512), 1) % 64
        fold_ref[...] = jnp.where(lane == expert_ref[...], 1.0, 0.0).astype(BF)
        u = lax.broadcasted_iota(jnp.int32, (512, 512), 0)
        t = lax.broadcasted_iota(jnp.int32, (512, 512), 1)
        same = jnp.logical_and(u // 128 == t // 128, u < t)
        before_ref[...] = jnp.where(same, 1.0, 0.0).astype(BF)

    col = col_ref[...].reshape(512, 640)
    spread = mm(wide_ref[...], col[:, 512:], ((1,), (1,)))
    row = lax.broadcasted_iota(jnp.int32, (512, 512), 0) % 64
    hit = spread[:512] == row.astype(F32)
    fold = fold_ref[...]
    named = mm(fold, jnp.where(hit, 1.0, 0.0).astype(BF))
    rank = mm(named.astype(BF), before_ref[...])
    send = jnp.logical_and(named > 0.5, rank == place_ref[...].astype(F32))
    parts = []
    for i in range(3):
        part = mm(fold, jnp.where(hit, spread[512 * (i + 1) : 512 * (i + 2)], 0.0).astype(BF))
        parts.append(jnp.where(send, part, 0.0).astype(BF))
    for j in range(4):
        one = [part[:, 128 * j : 128 * (j + 1)] for part in parts]
        hi_ref[j], mid_ref[j] = one[0], one[1]
        g = col[128 * j : 128 * (j + 1), :512]
        total = mm(jnp.concatenate(one, axis=1), jnp.concatenate([g, g, g], axis=0))
        for d, ref in enumerate((s0_ref, s1_ref, s2_ref, s3_ref)):
            ref[j] = total[PAIR * d : PAIR * (d + 1)].astype(BF)


def cotangent_rows(expert, place, column):
    rows = column.shape[1]
    step = lambda *shape: pl.BlockSpec((4,) + shape, lambda z: (z, 0, 0))
    const = pl.BlockSpec((160, 1), lambda z: (0, 0))
    sent = jax.ShapeDtypeStruct((8, PAIR, 512), BF)
    weight = jax.ShapeDtypeStruct((8, 160, rows), BF)
    return pl.pallas_call(
        cotangent_kernel,
        grid=(2,),
        in_specs=[const, const, step(rows, 640)],
        out_specs=[step(PAIR, 512)] * 4 + [step(160, rows)] * 2,
        out_shape=[sent] * 4 + [weight] * 2,
        scratch_shapes=[pltpu.VMEM((2048, 128), BF), pltpu.VMEM((160, 512), BF), pltpu.VMEM((512, 512), BF)],
        compiler_params=pltpu.CompilerParams(vmem_limit_bytes=32 * 1024 * 1024),
        cost_estimate=pl.CostEstimate(flops=1_000_000_000, bytes_accessed=3_000_000, transcendentals=0),
    )(expert, place, pltpu.with_memory_space_constraint(column, pltpu.HBM))


ORDER = (0, 3, 2, 1, 4)


def expert_block(x, g, w_up, w_down):
    pre = mm(x, w_up)
    grad_act = mm(g, w_down, ((1,), (1,)))
    gate, upper = pre[:, :512], pre[:, 512:]
    sigma = jax.nn.sigmoid(gate)
    soft = gate * sigma
    act = (soft * upper).astype(BF)
    grad_gate = (grad_act * upper * sigma * (1.0 + gate * (1.0 - sigma))).astype(BF)
    grad_up = (grad_act * soft).astype(BF)
    back = mm(jnp.concatenate([grad_gate, grad_up], axis=1), w_up, ((1,), (1,)))
    return back, mm(act, w_down)


def start(*groups):
    for copies in groups:
        for copy in copies:
            copy.start()


def wait(copies):
    for copy in copies:
        copy.wait()


def expert_kernel(
    x_ref, g_ref, up1, down1, up2, down2, back_ref, out_ref,
    x_in, g_in, back_to, out_to, up_ref, down_ref, w_sems, in_sems, out_sems
):
    weights = [
        [
            pltpu.make_async_copy(up, up_ref.at[e], w_sems.at[e, 0]),
            pltpu.make_async_copy(down, down_ref.at[e], w_sems.at[e, 1]),
        ]
        for e, (up, down) in enumerate(((up1, down1), (up2, down2)))
    ]
    rows, sent = [], []
    for n, b in enumerate(ORDER):
        part = (slice(None), pl.ds(16 * b, 16))
        rows.append([
            pltpu.make_async_copy(x_ref.at[part], x_in.at[n], in_sems.at[n, 0]),
            pltpu.make_async_copy(g_ref.at[part], g_in.at[n], in_sems.at[n, 1]),
        ])
        sent.append([
            pltpu.make_async_copy(back_to.at[n], back_ref.at[part], out_sems.at[n, 0]),
            pltpu.make_async_copy(out_to.at[n], out_ref.at[part], out_sems.at[n, 1]),
        ])
    start(rows[0], weights[0])

    def step(e, n):
        return expert_block(
            x_in[n].reshape(256, 512), g_in[n].reshape(256, 512), up_ref[e], down_ref[e]
        )

    wait(weights[0])
    start(*rows[1:], weights[1])
    for n in (0, 1):
        wait(rows[n])
        back, out = step(0, n)
        back_to[n] = back.astype(BF).reshape(16, 16, 512)
        out_to[n] = out.astype(BF).reshape(16, 16, 512)
        start(sent[n])
    wait(rows[2])
    own_back, own_out = step(0, 2)
    wait(weights[1])
    back, out = step(1, 2)
    keep = (lax.broadcasted_iota(jnp.int32, (256, 512), 0) % 8) < 4
    back_to[2] = jnp.where(keep, own_back, back).astype(BF).reshape(16, 16, 512)
    out_to[2] = jnp.where(keep, own_out, out).astype(BF).reshape(16, 16, 512)
    start(sent[2])
    for n in (3, 4):
        wait(rows[n])
        back, out = step(1, n)
        back_to[n] = back.astype(BF).reshape(16, 16, 512)
        out_to[n] = out.astype(BF).reshape(16, 16, 512)
        start(sent[n])
    for copies in sent:
        wait(copies)


def expert_rows(x, g, *weights):
    shape = pltpu.HBM((16, 80, 512), BF)
    hbm = lambda x: pltpu.with_memory_space_constraint(x, pltpu.HBM)
    block = pltpu.VMEM((5, 16, 16, 512), BF)
    back, out = pl.pallas_call(
        expert_kernel,
        in_specs=[pl.BlockSpec(memory_space=pl.ANY)] * 6,
        out_specs=[pl.BlockSpec(memory_space=pl.ANY)] * 2,
        out_shape=[shape, shape],
        scratch_shapes=[
            block,
            block,
            block,
            block,
            pltpu.VMEM((2, 512, 1024), BF),
            pltpu.VMEM((2, 512, 512), BF),
            pltpu.SemaphoreType.DMA((2, 2)),
            pltpu.SemaphoreType.DMA((5, 2)),
            pltpu.SemaphoreType.DMA((5, 2)),
        ],
        compiler_params=pltpu.CompilerParams(vmem_limit_bytes=40 * 1024 * 1024),
        cost_estimate=pl.CostEstimate(flops=4_800_000_000, bytes_accessed=8_500_000, transcendentals=800_000),
    )(x.reshape(16, 80, 512), hbm(g.reshape(16, 80, 512)), *map(hbm, weights))
    return back.reshape(32, PAIR, 512), out.reshape(32, PAIR, 512)


def three(x):
    high = x.astype(BF)
    mid = (x - high.astype(F32)).astype(BF)
    low = (x - high.astype(F32) - mid.astype(F32)).astype(BF)
    return high, mid, low


def named_in(routes):
    lanes = lax.broadcasted_iota(jnp.int32, (1,) * routes.ndim + (64,), routes.ndim)
    return routes[..., None] == lanes


def slot_code(named):
    rows = named.shape[-2]
    below = (
        lax.broadcasted_iota(jnp.int32, (rows, rows), 0)
        > lax.broadcasted_iota(jnp.int32, (rows, rows), 1)
    ).astype(BF)
    rank = jnp.einsum("ij,...je->...ie", below, named.astype(BF), preferred_element_type=F32)
    return jnp.where(named, rank, -1.0).astype(BF)


def slot_layout(q, at):
    q = (q + 32 * (at % 2)) % PAIR
    other = jnp.where(q < 2 * MAIN, q // MAIN, (q - 2 * MAIN) // (CAP - MAIN))
    place = jnp.where(q < 2 * MAIN, q % MAIN, MAIN + (q - 2 * MAIN) % (CAP - MAIN))
    return other, place


def shift_x(x, d):
    return lax.ppermute(x, "x", [(i, (i + d) % 4) for i in range(4)])


def take(x, i, axis):
    return lax.dynamic_index_in_dim(x, i, axis, keepdims=False)


def shards(tokens, routes, mix_weights, gate_up, down, w_in, grad_combined):
    rows = tokens.shape[0]
    gate_up, down = gate_up[0], down[0]
    core, at, plane = lax.axis_index("c"), lax.axis_index("x"), lax.axis_index("z")
    slots = 64 * CAP

    w_part = lax.all_to_all(
        jnp.broadcast_to(w_in[None], (64,) + w_in.shape), YZ, split_axis=0, concat_axis=0, tiled=True
    ).reshape(512, 512)

    payload = jnp.concatenate(
        [grad_combined, routes.astype(BF), *three(mix_weights), jnp.zeros((rows, 96), BF)], axis=1
    )
    column = lax.all_gather(payload, "z", axis=0, tiled=True).reshape(8, rows, 640)

    to = column_target(core, at)
    mine, theirs = split_columns(to, tokens)
    theirs = swap_core(theirs)
    both = jnp.stack([jnp.where(core == 0, mine, theirs), jnp.where(core == 0, theirs, mine)], axis=1)
    blocks = jnp.stack([both[0]] + [shift_x(both[d], d) for d in (1, 2, 3)])
    feature_block = jnp.stack([take(blocks, (at - j) % 4, 0) for j in range(4)])
    tokens_mine = take(feature_block, core, 1).reshape(4 * rows, 512)
    tokens_other = take(feature_block, 1 - core, 1).reshape(4 * rows, 512)

    gate_up2, down2 = swap_core(after(gate_up, w_part)), swap_core(after(down, w_part))
    w_both = jnp.concatenate([w_part, swap_core(w_part)])

    partial = mm(feature_block.reshape(8 * rows, 512), w_part).astype(BF).reshape(8, rows, 512)
    partials = lax.all_to_all(partial, XC, split_axis=0, concat_axis=0, tiled=True)

    r = lax.broadcasted_iota(jnp.int32, (4 * PAIR, 1), 0)
    other, place = slot_layout(r % PAIR, at)
    expert = plane * 8 + (at + r // PAIR) % 4 * 2 + (core + other) % 2
    *grad_send, weight_hi, weight_mid = cotangent_rows(expert, place, column)
    partials = after(partials, *grad_send)
    latent = jnp.sum(partials.astype(F32), axis=0).astype(BF)

    r = lax.broadcasted_iota(jnp.int32, (1, slots), 1)
    other, place = slot_layout(r % PAIR, at)
    spread = (
        lax.broadcasted_iota(jnp.int32, (64, slots), 0) == (r // PAIR) * 2 + (core + other) % 2
    ).astype(BF)
    code = slot_code(jnp.any(named_in(routes), axis=1))
    onehot = (mm(code, spread) == place.astype(F32)).astype(BF)
    out_send = mm(onehot, latent, ((0,), (0,))).astype(BF).reshape(32, PAIR, 512)
    out_send, w_both, *_ = lax.optimization_barrier(
        (out_send, w_both, gate_up2, down2, tokens_mine, tokens_other)
    )
    recv = lax.all_to_all(out_send, ZX, split_axis=0, concat_axis=0, tiled=True)

    sent = jnp.stack([grad_send[0]] + [shift_x(grad_send[d], d) for d in (1, 2, 3)])
    grad_recv = jnp.stack([take(sent, (at - j) % 4, 0) for j in range(4)], axis=1)

    grad_rows, outputs = expert_rows(recv, grad_recv, gate_up, down, gate_up2, down2)
    grad_back = lax.all_to_all(grad_rows, ZX, split_axis=0, concat_axis=0, tiled=True)

    out4 = outputs.reshape(8, 4, PAIR, 512)
    back = [take(out4, at, 1)] + [shift_x(take(out4, (at - d) % 4, 1), -d) for d in (1, 2, 3)]
    back = jnp.stack(back, axis=1).reshape(8, 4 * PAIR, 512)
    mixed = sum(
        jnp.einsum("zrt,zrl->ztl", w, back, preferred_element_type=F32) for w in (weight_hi, weight_mid)
    )
    mixed = mixed.reshape(8 * rows, 512)
    combined = lax.psum_scatter(mixed, "z", scatter_dimension=0, tiled=True).astype(BF)

    grad_back = after(grad_back, mixed)

    grad_latent = mm(onehot, grad_back.reshape(slots, 512)).astype(BF)
    line_grads = lax.all_gather(grad_latent, "x", axis=0, tiled=True)
    other_grads = swap_core(line_grads)
    first = ((0,), (0,))
    part = mm(tokens_mine, line_grads, first) + mm(tokens_other, other_grads, first)
    part = part.astype(BF).reshape(64, 8, 512)

    slices = mm(line_grads, w_both, ((1,), (1,))).astype(BF).reshape(4, rows, 1024)
    part = after(part, slices)
    parts = lax.all_to_all(part, YZ, split_axis=0, concat_axis=0, tiled=True)
    back = [take(slices, at, 0)] + [shift_x(take(slices, (at - d) % 4, 0), -d) for d in (1, 2, 3)]
    back[0] = after(back[0], parts)
    grad_tokens = join_columns(to, *back)
    grad_w_in = jnp.sum(parts.astype(F32), axis=0) / rows
    return combined, grad_tokens, grad_w_in


def solution(mesh):
    split = Mesh(mesh.devices.reshape(8, 8, 4, 2), ("dp", "z", "x", "c"))
    every = P(("dp", "z", "x", "c"), None)
    each = P(("z", "x", "c"), None, None)
    return jax.shard_map(
        shards,
        mesh=split,
        in_specs=(every, every, every, each, each, every, every),
        out_specs=(every, every, every),
        check_vma=False,
    )
```
